32 devices in a mesh: ctx: 4 (over y, x), ch: 8 (over z, core).
Axes of the slice: x: 2, y: 2, z: 4, core: 2. Of those that a mesh axis runs over, the one named last changes fastest.
Arguments:
- proj: bfloat16 [3, 4096, 1024], P(None, 'ch', 'ctx'), may hold values from -4 to 4
- scale_exp: int32 [3, 4096, 8], P(None, 'ch', 'ctx'), may hold values from -1 to 1
- filt: bfloat16 [4096, 1024], P('ch'), may hold values from -8 to 8
- reach: int32 [4096], P('ch'), may hold values from 0 to 4
- skip: float32 [4096], P('ch'), may hold values from 0.1 to 1.9
- cotangent: bfloat16 [4096, 1024], P('ch', 'ctx'), may hold values from -6 to 6
Outputs:
- scaled_out: bfloat16 [4096, 1024], P('ch', 'ctx')
- token_max: float32 [1024], P('ctx')
- gradients: bfloat16 [3, 4096, 1024], P(None, 'ch', 'ctx')
- filter_grad: float32 [4096, 1024], P('ch', 'ctx')
The draws below stay inside these ranges and needn't reach their ends.
All inputs are finite; a program needn't handle non-finite values. Where the reference program divides by a largest or mean magnitude, that divisor is 1e-20 or more.
Results may differ from the reference program's by a relative error of at most 0.015.
Values may be sent and summed in bfloat16 or wider, within the bound.
No kernel may reach another device: no remote copies, remote signals or barrier semaphores. Data moves between devices by JAX's collectives and lax.ppermute only.
A program may use at most 64 MiB of HBM per device.

```python
import math
import jax
import jax.numpy as jnp
from jax import lax

D = 4096
BLOCK = 128
SEQ = 1024


def draw_reach(key, part):
    raw_class = jax.random.randint(key, (D,), 0, 7, dtype=jnp.int32)
    return jnp.minimum(raw_class, 4)


def set_ends(entries, key, low, largest):
    shape = entries.shape
    index_at = [jax.random.randint(jax.random.fold_in(key, axis), (), 0, shape[axis]) for axis in range(len(shape))]
    entries = entries.at[tuple(index_at)].set(low)
    longest = shape.index(max(shape))
    index_at[longest] = (index_at[longest] + 1) % shape[longest]
    return entries.at[tuple(index_at)].set(largest)


def level_of(key, shape, shards, low, largest):
    loudness = 1.0
    for position, parts in shards:
        steps = jax.random.uniform(jax.random.fold_in(jax.random.fold_in(key, 6), position), (parts,), jnp.float32, low / len(shards), largest / len(shards))
        loudness = loudness * jnp.repeat(jnp.exp(steps), shape[position] // parts).reshape((-1,) + (1,) * (len(shape) - 1 - position))
    return loudness


def normal_values(own_key, shape, deviation, most, cuts=(), kind=jnp.bfloat16):
    values = jax.random.normal(own_key, shape, jnp.float32) * deviation
    if len(cuts) > 0:
        values = level_of(own_key, shape, cuts, -0.22, 0.18) * values
    return jnp.clip(values, min=-most, max=most).astype(kind)


def setup_inputs(seed: int = 0) -> dict:
    arg_keys = jax.random.split(jax.random.key(seed), 7)
    return {
        "proj": normal_values(arg_keys[0], (3, D, SEQ), 1.0, 4.0, ((1, 8), (2, 4))),
        "scale_exp": set_ends(jax.random.randint(arg_keys[1], (3, D, SEQ // BLOCK), -1, 2), jax.random.fold_in(arg_keys[1], 1), -1, 1).astype(jnp.int32),
        "filt": normal_values(arg_keys[2], (D, SEQ), 2.0, 8.0, ((0, 8),)),
        "reach": draw_reach(jax.random.fold_in(arg_keys[6], 71), 0),
        "skip": jnp.clip(1.0 + 0.18 * jax.random.normal(arg_keys[4], (D,), jnp.float32), 0.1, 1.9),
        "cotangent": normal_values(arg_keys[5], (D, SEQ), 1.0, 6.0, ((0, 8), (1, 4))),
    }


REACH_DIVISORS = (64, 32, 16, 4, 1)

def reference(proj, scale_exp, filt, reach, skip, cotangent):
    groups, channels, length = proj.shape
    scaled = jnp.exp2(scale_exp.astype(jnp.float32))
    dequant = (proj.astype(jnp.float32).reshape(groups, channels, length // BLOCK, BLOCK) * scaled[..., None]).reshape(groups, channels, length)
    queries = dequant[0]
    keys_deq = dequant[1]
    values_deq = dequant[2]
    mixed_bf = (keys_deq * values_deq).astype(jnp.bfloat16)
    mixed_f = lax.optimization_barrier(mixed_bf).astype(jnp.float32)
    divisors = jnp.array(REACH_DIVISORS, dtype=jnp.int32)
    reach_len = (SEQ // jnp.take(divisors, reach)).astype(jnp.int32)
    tap_index = jnp.arange(SEQ, dtype=jnp.int32)
    in_reach = (tap_index[None, :] < reach_len[:, None]).astype(jnp.float32)
    fscale = 1.0 / math.sqrt(SEQ)
    kernel = filt.astype(jnp.float32) * fscale * in_reach
    doubled = 2 * SEQ
    mixed_spec = jnp.fft.rfft(mixed_f, n=doubled, axis=1)
    kernel_spec = jnp.fft.rfft(kernel, n=doubled, axis=1)
    conv_out = jnp.fft.irfft(mixed_spec * kernel_spec, n=doubled, axis=1)[:, :SEQ] + skip[:, None] * mixed_f
    response = queries * conv_out
    token_max = lax.optimization_barrier(jnp.max(jnp.abs(response), axis=0))
    scaled_out = (response / (token_max + 1e-06)[None, :]).astype(jnp.bfloat16)
    upstream = cotangent.astype(jnp.float32)
    pulled_bf = (upstream * queries).astype(jnp.bfloat16)
    pulled = lax.optimization_barrier(pulled_bf).astype(jnp.float32)
    pulled_spec = jnp.fft.rfft(pulled, n=doubled, axis=1)
    grad_mixed = jnp.fft.irfft(jnp.conj(kernel_spec) * pulled_spec, n=doubled, axis=1)[:, :SEQ] + skip[:, None] * pulled
    gradients = jnp.stack([upstream * conv_out, grad_mixed * values_deq, grad_mixed * keys_deq]).astype(jnp.bfloat16)
    filter_grad = jnp.fft.irfft(jnp.conj(mixed_spec) * pulled_spec, n=doubled, axis=1)[:, :SEQ] * fscale * in_reach
    return (scaled_out, token_max, gradients, filter_grad)
```

```python
import functools
import math

import jax
import jax.numpy as jnp
import ml_dtypes
import numpy as np
from jax import lax
from jax.experimental import pallas as pl
from jax.experimental.pallas import tpu as pltpu
from jax.sharding import PartitionSpec as P

REACH_DIVISORS = (64, 32, 16, 4, 1)
F32 = jnp.float32
BF16 = jnp.bfloat16


def fourier_tables(span):
    freq = np.arange(span)
    time = np.arange(2 * span)
    phase = ((2 * freq[None, :] + 1) * time[:, None]) % (4 * span)
    angle = phase * (math.pi / (2 * span))
    forward = np.concatenate([np.cos(angle), -np.sin(angle)], axis=1)
    high = forward.astype(ml_dtypes.bfloat16)
    low = (forward - high.astype(np.float64)).astype(ml_dtypes.bfloat16)
    inverse = (forward.T / span).astype(ml_dtypes.bfloat16)
    return high, low, inverse


def mm(left, right):
    return lax.dot_general(left, right, (((1,), (0,)), ((), ())), preferred_element_type=F32)


def mm2(left, high, low):
    return mm(left, high) + mm(left, low)


def block_scale(exps, span):
    blocks = exps.shape[0]
    block_len = span // blocks
    col = lax.broadcasted_iota(jnp.int32, (blocks, span), 1)
    row = lax.broadcasted_iota(jnp.int32, (blocks, span), 0)
    onehot = jnp.where(col // block_len == row, 1.0, 0.0).astype(BF16)
    scale = jnp.exp2(exps.astype(F32)).astype(BF16)
    return lax.dot_general(scale, onehot, (((0,), (0,)), ((), ())), preferred_element_type=F32)


def column(row_ref):
    row = row_ref[...]
    return jnp.transpose(jnp.broadcast_to(row, (8, row.shape[1])))[:, 0:1]


def reach_lens(reach_ref, seq_len):
    cls = column(reach_ref)
    out = jnp.zeros_like(cls)
    for index, div in enumerate(REACH_DIVISORS):
        out = jnp.where(cls == index, seq_len // div, out)
    return out


def cmul_parts(first, second, half):
    ar, ai = first[:, :half], first[:, half:]
    br, bi = second[:, :half], second[:, half:]
    return ar, ai, br, bi


def prep_kernel(n, proj_ref, exp_ref, cot_ref, mixed_ref, pulled_ref, *send_refs):
    me = lax.axis_index("ctx")
    span = cot_ref.shape[1]
    exps = exp_ref[...]
    mixed = (
        proj_ref[1].astype(F32) * proj_ref[2].astype(F32) * block_scale(exps[1] + exps[2], span)
    ).astype(BF16)
    pulled = (cot_ref[...].astype(F32) * (proj_ref[0].astype(F32) * block_scale(exps[0], span))).astype(BF16)
    mixed_ref[...] = mixed
    pulled_ref[...] = pulled
    for bit, ref in enumerate(send_refs):
        later = lax.rem(lax.div(me, 2**bit), 2)

        @pl.when(later == 1)
        def _():
            ref[...] = pulled

        @pl.when(later == 0)
        def _():
            ref[...] = mixed


def windows_kernel(
    n, proj_ref, exp_ref, filt_ref, reach_ref, skip_ref, mixed_ref, pulled_ref, high_ref, low_ref,
    recv_ref, query_ref, base_ref, *rest
):
    win_refs, taps = rest[: n - 2], rest[n - 2]
    me = lax.axis_index("ctx")
    rows, seq_len = filt_ref.shape
    span = seq_len // n
    fscale = 1.0 / math.sqrt(seq_len)
    query_ref[...] = (proj_ref[...].astype(F32) * block_scale(exp_ref[...], span)).astype(BF16)
    lens = reach_lens(reach_ref, seq_len)
    taps[0] = jnp.zeros((rows, span), BF16)
    for b in range(n):
        lag = lax.broadcasted_iota(jnp.int32, (rows, span), 1) + b * span
        taps[b + 1] = jnp.where(lag < lens, filt_ref[:, b * span : (b + 1) * span].astype(F32), 0.0).astype(BF16)
    near = mm2(taps[1], high_ref[span:], low_ref[span:])
    near += (column(skip_ref) * (1.0 / fscale)) * high_ref[span : span + 1, :].astype(F32)
    wr, wi = near[:, :span], near[:, span:]
    own = mm2(mixed_ref[...], high_ref[:span], low_ref[:span])
    xr, xi = own[:, :span], own[:, span:]
    base_ref[0, :, :span] = xr * wr - xi * wi
    base_ref[0, :, span:] = xr * wi + xi * wr
    back = mm2(pulled_ref[...], high_ref[span:], low_ref[span:])
    xr, xi = back[:, :span], back[:, span:]
    base_ref[1, :, :span] = xr * wr + xi * wi
    base_ref[1, :, span:] = xi * wr - xr * wi
    for k in range(1, n):
        other = jnp.bitwise_xor(me, k)
        dist = jnp.abs(other - me)
        win = mm2(taps[dist], high_ref[:span], low_ref[:span]) + mm2(
            taps[dist + 1], high_ref[span:], low_ref[span:]
        )
        sign = jnp.where(other < me, 1.0, -1.0).astype(F32)
        wr, wi = win[:, :span], win[:, span:] * sign
        if k > 1:
            win_refs[k - 2][:, :span] = wr.astype(BF16)
            win_refs[k - 2][:, span:] = wi.astype(BF16)
            continue
        later = jnp.where(other > me, 1, 0)
        start = pl.multiple_of(later * span, span)
        spec = mm2(recv_ref[...], high_ref[pl.ds(start, span), :], low_ref[pl.ds(start, span), :])
        xr, xi = spec[:, :span], spec[:, span:]
        base_ref[later, :, :span] += xr * wr - xi * wi
        base_ref[later, :, span:] += xr * wi + xi * wr


def conv_kernel(n, seq_len, *refs):
    recv_refs, win_refs = refs[: n - 2], refs[n - 2 : 2 * n - 4]
    base_ref, query_ref, high_ref, inv_ref = refs[2 * n - 4 : 2 * n]
    resp_ref, conv_ref, back_ref, peak_ref, acc = refs[2 * n :]
    me = lax.axis_index("ctx")
    span = query_ref.shape[1]
    fscale = 1.0 / math.sqrt(seq_len)
    acc[...] = base_ref[...]
    for k in range(2, n):
        later = jnp.where(jnp.bitwise_xor(me, k) > me, 1, 0)
        start = pl.multiple_of(later * span, span)
        spec = mm(recv_refs[k - 2][...], high_ref[pl.ds(start, span), :])
        xr, xi = spec[:, :span], spec[:, span:]
        wr = win_refs[k - 2][:, :span].astype(F32)
        wi = win_refs[k - 2][:, span:].astype(F32)
        acc[later, :, :span] += xr * wr - xi * wi
        acc[later, :, span:] += xr * wi + xi * wr
    conv = mm(acc[0].astype(BF16), inv_ref[:, span:]) * fscale
    response = query_ref[...].astype(F32) * conv
    resp_ref[...] = response
    conv_ref[...] = conv
    back_ref[...] = acc[1].astype(BF16)
    peak = jnp.max(jnp.abs(response), axis=0, keepdims=True)

    @pl.when(pl.program_id(0) == 0)
    def _():
        peak_ref[...] = peak

    @pl.when(pl.program_id(0) > 0)
    def _():
        peak_ref[...] = jnp.maximum(peak_ref[...], peak)


def grad_kernel(seq_len, key_ref, value_ref, exp_ref, cot_ref, conv_ref, back_ref, inv_ref, grad_ref):
    span = cot_ref.shape[1]
    fscale = 1.0 / math.sqrt(seq_len)
    exps = exp_ref[...]
    grad_mixed = mm(back_ref[...], inv_ref[:, :span]) * fscale
    grad_ref[0] = (cot_ref[...].astype(F32) * conv_ref[...]).astype(BF16)
    grad_ref[1] = (grad_mixed * (value_ref[...].astype(F32) * block_scale(exps[2], span))).astype(BF16)
    grad_ref[2] = (grad_mixed * (key_ref[...].astype(F32) * block_scale(exps[1], span))).astype(BF16)


def taps_kernel(n, seq_len, mixed_ref, pulled_ref, reach_ref, high_ref, inv_ref, *refs):
    first_refs, second_refs = refs[: n - 1], refs[n - 1 : 2 * n - 2]
    out_refs, (mbuf, pbuf, mspec, pspec, acc) = refs[2 * n - 1 : 3 * n - 1], refs[3 * n - 1 :]
    me = lax.axis_index("ctx")
    _, rows, span = mbuf.shape
    fscale = 1.0 / math.sqrt(seq_len)
    mbuf[me] = mixed_ref[me]
    pbuf[me] = pulled_ref[me]
    pbuf[n] = jnp.zeros((rows, span), BF16)
    for k in range(1, n):
        other = jnp.bitwise_xor(me, k)

        @pl.when(other < me)
        def _():
            mbuf[other] = first_refs[k - 1][me]
            pbuf[other] = second_refs[k - 1][...]

        @pl.when(other > me)
        def _():
            pbuf[other] = first_refs[k - 1][me]
            mbuf[other] = second_refs[k - 1][...]

    if rows % 16 == 0:
        flat = (n * rows, span)
        mspec[...] = mm(mbuf[...].reshape(flat), high_ref[:span]).reshape(mspec.shape)
        pspec[...] = (
            mm(pbuf[:n].reshape(flat), high_ref[:span]) + mm(pbuf[1:].reshape(flat), high_ref[span:])
        ).reshape(pspec.shape)
    else:
        for b in range(n):
            mspec[b] = mm(mbuf[b], high_ref[:span])
            pspec[b] = mm(pbuf[b], high_ref[:span]) + mm(pbuf[b + 1], high_ref[span:])
    lens = reach_lens(reach_ref.at[me], seq_len)
    for k in range(n):
        lag_block = jnp.bitwise_xor(me, k)
        acc[...] = jnp.zeros_like(acc)
        for b in range(n):

            @pl.when(b + lag_block < n)
            def _():
                ar, ai = mspec[b, :, :span], mspec[b, :, span:]
                near = pspec[b + lag_block]
                br, bi = near[:, :span], near[:, span:]
                acc[:, :span] += ar * br + ai * bi
                acc[:, span:] += ar * bi - ai * br

        lag = lax.broadcasted_iota(jnp.int32, (rows, span), 1) + lag_block * span
        own = mm(acc[...].astype(BF16), inv_ref[:, :span]) * fscale
        out_refs[k][...] = jnp.where(lag < lens, own, 0.0).astype(BF16)


def pick_kernel(k, mixed_ref, pulled_ref, *refs):
    me = lax.axis_index("ctx")
    other = jnp.bitwise_xor(me, k)
    out_ref = refs[-1]

    @pl.when(other > me)
    def _():
        out_ref[...] = pulled_ref[other]

    @pl.when(other < me)
    def _():
        out_ref[...] = mixed_ref[other]


def spread_kernel(n, *refs):
    part_refs, out_ref = refs[:n], refs[n]
    me = lax.axis_index("ctx")
    for k in range(n):
        out_ref[jnp.bitwise_xor(me, k)] = part_refs[k][...].astype(F32)


def scale_kernel(resp_ref, near_ref, far_ref, out_ref, peak_ref):
    peak = jnp.maximum(near_ref[...], far_ref[...])
    peak_ref[...] = peak
    out_ref[...] = (resp_ref[...] / (peak + 1e-06)).astype(BF16)


def params(mib=40):
    return pltpu.CompilerParams(vmem_limit_bytes=mib * 2**20)


def body(proj, scale_exp, filt, reach, skip, cotangent):
    groups, channels, span = proj.shape
    n = lax.axis_size("ctx")
    ch_count = lax.axis_size("ch")
    seq_len = n * span
    blocks = scale_exp.shape[2]
    bits = max(1, (n - 1).bit_length())
    rows = 256 if channels % 256 == 0 else channels
    steps = channels // rows
    high, low, inverse = (jnp.asarray(t) for t in fourier_tables(span))
    exps = jnp.transpose(scale_exp, (0, 2, 1))
    reach_row = reach.reshape(1, channels)
    skip_row = skip.reshape(1, channels)

    tile = pl.BlockSpec((rows, span), lambda i: (i, 0))
    wide = pl.BlockSpec((rows, 2 * span), lambda i: (i, 0))
    line = pl.BlockSpec((1, rows), lambda i: (0, i))
    table = pl.BlockSpec((2 * span, 2 * span), lambda i: (0, 0))
    proj_all = pl.BlockSpec((3, rows, span), lambda i: (0, i, 0))
    exps_all = pl.BlockSpec((3, blocks, rows), lambda i: (0, 0, i))

    def shape(dims, dtype):
        return jax.ShapeDtypeStruct(dims, dtype)

    flat = shape((channels, span), BF16)
    mixed, pulled, *sends = pl.pallas_call(
        functools.partial(prep_kernel, n),
        grid=(steps,),
        in_specs=[proj_all, exps_all, tile],
        out_specs=[tile] * (2 + bits),
        out_shape=[flat] * (2 + bits),
        compiler_params=params(60),
        name="prep",
    )(proj, exps, cotangent)

    first = []
    for k in range(1, n):
        perm = [(j, j ^ k) for j in range(n)]
        first.append(lax.ppermute(sends[k.bit_length() - 1], "ctx", perm))
    me = lax.axis_index("ctx")
    share = channels // n
    shares = (n, share, span)
    part = shape((share, span), BF16)

    def pick(k, *after):
        return pl.pallas_call(
            functools.partial(pick_kernel, k),
            in_specs=[pl.BlockSpec(memory_space=pltpu.VMEM)] * 2 + [pl.BlockSpec(memory_space=pl.ANY)] * len(after),
            out_shape=part,
            compiler_params=params(),
            name="pick",
        )(mixed.reshape(shares), pulled.reshape(shares), *after)

    second = {k: lax.ppermute(pick(k), "ctx", [(j, j ^ k) for j in range(n)]) for k in range(2, n)}

    query, base, *wins = pl.pallas_call(
        functools.partial(windows_kernel, n),
        grid=(steps,),
        in_specs=[
            pl.BlockSpec((None, rows, span), lambda i: (0, i, 0)),
            pl.BlockSpec((None, blocks, rows), lambda i: (0, 0, i)),
            pl.BlockSpec((rows, seq_len), lambda i: (i, 0)),
            line, line, tile, tile, table, table, tile,
        ],
        out_specs=[tile, pl.BlockSpec((2, rows, 2 * span), lambda i: (0, i, 0))] + [wide] * (n - 2),
        out_shape=[flat, shape((2, channels, 2 * span), F32)] + [shape((channels, 2 * span), BF16)] * (n - 2),
        scratch_shapes=[pltpu.VMEM((n + 1, rows, span), BF16)],
        compiler_params=params(),
        name="windows",
    )(proj, exps, filt, reach_row, skip_row, mixed, pulled, high, low, first[0])
    second[1] = lax.ppermute(pick(1, first[0]), "ctx", [(j, j ^ 1) for j in range(n)])

    response, conv, back, peak = pl.pallas_call(
        functools.partial(conv_kernel, n, seq_len),
        grid=(steps,),
        in_specs=[tile] * (n - 2) + [wide] * (n - 2)
        + [pl.BlockSpec((2, rows, 2 * span), lambda i: (0, i, 0)), tile, table, table],
        out_specs=[tile, tile, wide, pl.BlockSpec((1, span), lambda i: (0, 0))],
        out_shape=[shape((channels, span), F32)] * 2
        + [shape((channels, 2 * span), BF16), shape((1, span), F32)],
        scratch_shapes=[pltpu.VMEM((2, rows, 2 * span), F32)],
        compiler_params=params(),
        name="conv",
    )(*first[1:], *wins, base, query, high, inverse)

    far = peak
    hop = 1
    while hop < ch_count:
        peak = jnp.maximum(peak, far)
        far = lax.ppermute(peak, "ch", [(j, j ^ hop) for j in range(ch_count)])
        hop *= 2
    single = pl.BlockSpec((1, span), lambda i: (0, 0))
    scaled_out, peak = pl.pallas_call(
        scale_kernel,
        grid=(steps,),
        in_specs=[tile, single, single],
        out_specs=[tile, single],
        out_shape=[flat, shape((1, span), F32)],
        compiler_params=params(),
        name="scale",
    )(response, peak, far)

    gradients = pl.pallas_call(
        functools.partial(grad_kernel, seq_len),
        grid=(steps,),
        in_specs=[
            pl.BlockSpec((None, rows, span), lambda i: (1, i, 0)),
            pl.BlockSpec((None, rows, span), lambda i: (2, i, 0)),
            exps_all, tile, tile, wide, table,
        ],
        out_specs=proj_all,
        out_shape=shape((3, channels, span), BF16),
        compiler_params=params(),
        name="grads",
    )(proj, proj, exps, cotangent, conv, back, inverse)

    own_part, *parts = pl.pallas_call(
        functools.partial(taps_kernel, n, seq_len),
        in_specs=[pl.BlockSpec(memory_space=pltpu.VMEM)] * (2 * n + 3) + [pl.BlockSpec(memory_space=pl.ANY)],
        out_shape=[part] * n,
        scratch_shapes=[
            pltpu.VMEM(shares, BF16),
            pltpu.VMEM((n + 1, share, span), BF16),
            pltpu.VMEM((n, share, 2 * span), F32),
            pltpu.VMEM((n, share, 2 * span), F32),
            pltpu.VMEM((share, 2 * span), F32),
        ],
        compiler_params=params(),
        name="taps",
    )(
        mixed.reshape(shares), pulled.reshape(shares), reach.reshape(n, 1, share), high, inverse,
        *[x.reshape(shares) for x in first], *[second[k] for k in range(1, n)], peak,
    )
    parts = [
        lax.ppermute(x, "ctx", [(j, j ^ (k + 1)) for j in range(n)]) for k, x in enumerate(parts)
    ]
    filter_grad = pl.pallas_call(
        functools.partial(spread_kernel, n),
        out_shape=shape(shares, F32),
        compiler_params=params(),
        name="spread",
    )(own_part, *parts).reshape(channels, span)
    return (scaled_out, peak.reshape(span), gradients, filter_grad)


def solution(mesh):
    return jax.shard_map(
        body,
        mesh=mesh,
        in_specs=(
            P(None, "ch", "ctx"),
            P(None, "ch", "ctx"),
            P("ch", None),
            P("ch"),
            P("ch"),
            P("ch", "ctx"),
        ),
        out_specs=(P("ch", "ctx"), P("ctx"), P(None, "ch", "ctx"), P("ch", "ctx")),
        check_vma=False,
    )
```

```python
import functools
import math

import jax
import jax.numpy as jnp
import ml_dtypes
import numpy as np
from jax import lax
from jax.experimental import pallas as pl
from jax.experimental.pallas import tpu as pltpu
from jax.sharding import PartitionSpec as P

REACH_DIVISORS = (64, 32, 16, 4, 1)
F32 = jnp.float32
BF16 = jnp.bfloat16


def fourier_tables(span):
    freq = np.arange(span)
    time = np.arange(2 * span)
    phase = ((2 * freq[None, :] + 1) * time[:, None]) % (4 * span)
    angle = phase * (math.pi / (2 * span))
    forward = np.concatenate([np.cos(angle), -np.sin(angle)], axis=1)
    high = forward.astype(ml_dtypes.bfloat16)
    low = (forward - high.astype(np.float64)).astype(ml_dtypes.bfloat16)
    inverse = (forward.T / span).astype(ml_dtypes.bfloat16)
    return high, low, inverse


def mm(left, right):
    return lax.dot_general(left, right, (((1,), (0,)), ((), ())), preferred_element_type=F32)


def mm2(left, high, low):
    return mm(left, high) + mm(left, low)


def block_scale(exps, span):
    blocks = exps.shape[0]
    block_len = span // blocks
    col = lax.broadcasted_iota(jnp.int32, (blocks, span), 1)
    row = lax.broadcasted_iota(jnp.int32, (blocks, span), 0)
    onehot = jnp.where(col // block_len == row, 1.0, 0.0).astype(BF16)
    scale = jnp.exp2(exps.astype(F32)).astype(BF16)
    return lax.dot_general(scale, onehot, (((0,), (0,)), ((), ())), preferred_element_type=F32)


def column(row_ref):
    row = row_ref[...]
    return jnp.transpose(jnp.broadcast_to(row, (8, row.shape[1])))[:, 0:1]


def reach_lens(reach_ref, seq_len):
    cls = column(reach_ref)
    out = jnp.zeros_like(cls)
    for index, div in enumerate(REACH_DIVISORS):
        out = jnp.where(cls == index, seq_len // div, out)
    return out


def cmul_parts(first, second, half):
    ar, ai = first[:, :half], first[:, half:]
    br, bi = second[:, :half], second[:, half:]
    return ar, ai, br, bi


def row_loop(total, step):
    def run(step_fn):
        if total <= step:
            step_fn(slice(0, total))
            return

        def one(i, carry):
            step_fn(pl.ds(pl.multiple_of(i * step, step), step))
            return carry

        lax.fori_loop(0, total // step, one, 0)

    return run


def top_bit(n):
    return lax.div(lax.axis_index("ctx"), (n + 1) // 2)


def prep_kernel(parts, n, proj_hbm, exp_hbm, cot_hbm, main_ref, rest_ref, *refs):
    send_refs, (proj, exp, cot, exp_sem, key_sem, query_sem) = refs[:-6], refs[-6:]
    me = lax.axis_index("ctx")
    upper = top_bit(n)
    channels, span = cot.shape
    rows = channels // parts
    exp_copy = pltpu.make_async_copy(exp_hbm, exp, exp_sem)
    exp_copy.start()
    copies = []
    for part in range(parts):
        block = pl.ds(part * rows, rows)
        copies.append(
            (
                pltpu.make_async_copy(proj_hbm.at[1, block], proj.at[1, block], key_sem.at[part, 0]),
                pltpu.make_async_copy(proj_hbm.at[2, block], proj.at[2, block], key_sem.at[part, 1]),
                pltpu.make_async_copy(proj_hbm.at[0, block], proj.at[0, block], query_sem.at[part, 0]),
                pltpu.make_async_copy(cot_hbm.at[block], cot.at[block], query_sem.at[part, 1]),
            )
        )
        for copy in copies[-1]:
            copy.start()
    exp_copy.wait()
    exps = exp[...]
    for part in range(parts):
        block = pl.ds(part * rows, rows)
        key_scale = block_scale(exps[1, :, part * rows : (part + 1) * rows] + exps[2, :, part * rows : (part + 1) * rows], span)
        query_scale = block_scale(exps[0, :, part * rows : (part + 1) * rows], span)
        for copy in copies[part]:
            copy.wait()
        mixed = (proj[1, block].astype(F32) * proj[2, block].astype(F32) * key_scale).astype(BF16)
        pulled = (cot[block].astype(F32) * (proj[0, block].astype(F32) * query_scale)).astype(BF16)
        lows = [lax.rem(lax.div(me, 2**bit), 2) for bit in range(len(send_refs))]
        for ref, later in [(main_ref, upper), (rest_ref, 1 - upper), *zip(send_refs, lows)]:

            @pl.when(later == 1)
            def _():
                ref[block] = pulled

            @pl.when(later == 0)
            def _():
                ref[block] = mixed


def windows_kernel(
    n, rows, proj_ref, exp_ref, filt_ref, reach_ref, skip_ref, main_ref, rest_ref, high_ref, low_ref,
    recv_ref, query_ref, base_ref, *rest
):
    win_refs, (taps, lens, gain) = rest[: n - 2], rest[n - 2 :]
    me = lax.axis_index("ctx")
    channels, seq_len = filt_ref.shape
    span = seq_len // n
    fscale = 1.0 / math.sqrt(seq_len)
    query_ref[...] = (proj_ref[0].astype(F32) * block_scale(exp_ref[0], span)).astype(BF16)
    upper = top_bit(n)
    lens[...] = reach_lens(reach_ref, seq_len)
    gain[...] = column(skip_ref) * (1.0 / fscale)

    @row_loop(channels, rows)
    def _(block):
        count = min(rows, channels)
        taps[0] = jnp.zeros((count, span), BF16)
        for b in range(n):
            lag = lax.broadcasted_iota(jnp.int32, (count, span), 1) + b * span
            taps[b + 1] = jnp.where(
                lag < lens[block], filt_ref[block, b * span : (b + 1) * span].astype(F32), 0.0
            ).astype(BF16)
        near = mm2(taps[1], high_ref[span:], low_ref[span:])
        near += gain[block] * high_ref[span : span + 1, :].astype(F32)
        wr, wi = near[:, :span], near[:, span:]
        for ref, later in ((main_ref, upper), (rest_ref, 1 - upper)):
            start = pl.multiple_of(later * span, span)
            spec = mm2(ref[block], high_ref[pl.ds(start, span), :], low_ref[pl.ds(start, span), :])
            xr, xi = spec[:, :span], spec[:, span:]
            turned = wi * (1 - 2 * later).astype(F32)
            base_ref[later, block, :span] = xr * wr - xi * turned
            base_ref[later, block, span:] = xr * turned + xi * wr
        for k in range(1, n):
            other = jnp.bitwise_xor(me, k)
            dist = jnp.abs(other - me)
            win = mm2(taps[dist], high_ref[:span], low_ref[:span]) + mm2(
                taps[dist + 1], high_ref[span:], low_ref[span:]
            )
            sign = jnp.where(other < me, 1.0, -1.0).astype(F32)
            wr, wi = win[:, :span], win[:, span:] * sign
            if k > 1:
                win_refs[k - 2][block, :span] = wr.astype(BF16)
                win_refs[k - 2][block, span:] = wi.astype(BF16)
                continue
            later = jnp.where(other > me, 1, 0)
            start = pl.multiple_of(later * span, span)
            spec = mm2(recv_ref[block], high_ref[pl.ds(start, span), :], low_ref[pl.ds(start, span), :])
            xr, xi = spec[:, :span], spec[:, span:]
            base_ref[later, block, :span] += xr * wr - xi * wi
            base_ref[later, block, span:] += xr * wi + xi * wr


def conv_kernel(n, seq_len, rows, *refs):
    recv_refs, win_refs = refs[: n - 2], refs[n - 2 : 2 * n - 4]
    _, query_ref, high_ref, inv_ref = refs[2 * n - 4 : 2 * n]
    acc, resp_ref, conv_ref, peak_ref = refs[2 * n :]
    me = lax.axis_index("ctx")
    channels, span = query_ref.shape
    fscale = 1.0 / math.sqrt(seq_len)
    peak_ref[...] = jnp.zeros_like(peak_ref)

    @row_loop(channels, rows)
    def _(block):
        for k in range(2, n):
            later = jnp.where(jnp.bitwise_xor(me, k) > me, 1, 0)
            start = pl.multiple_of(later * span, span)
            spec = mm(recv_refs[k - 2][block], high_ref[pl.ds(start, span), :])
            xr, xi = spec[:, :span], spec[:, span:]
            wr = win_refs[k - 2][block, :span].astype(F32)
            wi = win_refs[k - 2][block, span:].astype(F32)
            acc[later, block, :span] += xr * wr - xi * wi
            acc[later, block, span:] += xr * wi + xi * wr
        conv = mm(acc[0, block].astype(BF16), inv_ref[:, span:]) * fscale
        response = query_ref[block].astype(F32) * conv
        resp_ref[block] = response
        conv_ref[block] = conv
        peak_ref[...] = jnp.maximum(peak_ref[...], jnp.max(jnp.abs(response), axis=0, keepdims=True))


def grad_kernel(seq_len, rows, proj_ref, exp_ref, cot_ref, conv_ref, acc_ref, inv_ref, grad_ref):
    channels, span = cot_ref.shape
    fscale = 1.0 / math.sqrt(seq_len)
    exps = exp_ref[...]
    grad_mixed = mm(acc_ref[1].astype(BF16), inv_ref[:, :span]) * fscale
    grad_ref[0] = (cot_ref[...].astype(F32) * conv_ref[...]).astype(BF16)
    grad_ref[1] = (grad_mixed * (proj_ref[2].astype(F32) * block_scale(exps[2], span))).astype(BF16)
    grad_ref[2] = (grad_mixed * (proj_ref[1].astype(F32) * block_scale(exps[1], span))).astype(BF16)


def taps_kernel(n, seq_len, main_ref, rest_ref, reach_ref, high_ref, inv_ref, *refs):
    first_refs, second_refs, refs = refs[: n - 1], refs[n - 1 : 2 * n - 2], refs[2 * n - 2 :]
    peak_ref, out_refs, top_ref = refs[0], refs[1 : n + 1], refs[n + 1]
    mbuf, pbuf, mspec, pspec, acc = refs[n + 2 :]
    top_ref[...] = peak_ref[...]
    me = lax.axis_index("ctx")
    _, rows, span = mbuf.shape
    fscale = 1.0 / math.sqrt(seq_len)
    upper = top_bit(n)

    @pl.when(upper == 0)
    def _():
        mbuf[me] = main_ref[me]
        pbuf[me] = rest_ref[me]

    @pl.when(upper == 1)
    def _():
        mbuf[me] = rest_ref[me]
        pbuf[me] = main_ref[me]

    pbuf[n] = jnp.zeros((rows, span), BF16)
    for k in range(1, n):
        other = jnp.bitwise_xor(me, k)

        @pl.when(other < me)
        def _():
            mbuf[other] = first_refs[k - 1][me]
            pbuf[other] = second_refs[k - 1][...]

        @pl.when(other > me)
        def _():
            pbuf[other] = first_refs[k - 1][me]
            mbuf[other] = second_refs[k - 1][...]

    if rows % 16 == 0:
        flat = (n * rows, span)
        mspec[...] = mm(mbuf[...].reshape(flat), high_ref[:span]).reshape(mspec.shape)
        pspec[...] = (
            mm(pbuf[:n].reshape(flat), high_ref[:span]) + mm(pbuf[1:].reshape(flat), high_ref[span:])
        ).reshape(pspec.shape)
    else:
        for b in range(n):
            mspec[b] = mm(mbuf[b], high_ref[:span])
            pspec[b] = mm(pbuf[b], high_ref[:span]) + mm(pbuf[b + 1], high_ref[span:])
    lens = reach_lens(reach_ref.at[me], seq_len)
    for k in range(n):
        lag_block = jnp.bitwise_xor(me, k)
        acc[...] = jnp.zeros_like(acc)
        for b in range(n):

            @pl.when(b + lag_block < n)
            def _():
                ar, ai = mspec[b, :, :span], mspec[b, :, span:]
                near = pspec[b + lag_block]
                br, bi = near[:, :span], near[:, span:]
                acc[:, :span] += ar * br + ai * bi
                acc[:, span:] += ar * bi - ai * br

        lag = lax.broadcasted_iota(jnp.int32, (rows, span), 1) + lag_block * span
        own = mm(acc[...].astype(BF16), inv_ref[:, :span]) * fscale
        out_refs[k][...] = jnp.where(lag < lens, own, 0.0).astype(BF16)


def pick_kernel(k, n, main_ref, rest_ref, *refs):
    me = lax.axis_index("ctx")
    other = jnp.bitwise_xor(me, k)
    out_ref = refs[-1]

    wanted = jnp.where(other > me, 1, 0)

    @pl.when(wanted == top_bit(n))
    def _():
        out_ref[...] = main_ref[other]

    @pl.when(wanted != top_bit(n))
    def _():
        out_ref[...] = rest_ref[other]


def spread_kernel(n, *refs):
    part_refs, out_ref = refs[:n], refs[n]
    me = lax.axis_index("ctx")
    for k in range(n):
        out_ref[jnp.bitwise_xor(me, k)] = part_refs[k][...].astype(F32)


def scale_kernel(resp_ref, near_ref, far_ref, out_ref, peak_ref):
    peak = jnp.maximum(near_ref[...], far_ref[...])
    peak_ref[...] = peak
    out_ref[...] = (resp_ref[...] / (peak + 1e-06)).astype(BF16)


def params(mib=32):
    return pltpu.CompilerParams(vmem_limit_bytes=mib * 2**20)


def body(proj, scale_exp, filt, reach, skip, cotangent):
    groups, channels, span = proj.shape
    n = lax.axis_size("ctx")
    ch_count = lax.axis_size("ch")
    seq_len = n * span
    blocks = scale_exp.shape[2]
    bits = max(1, (n - 1).bit_length())
    rows = 256 if channels % 256 == 0 else channels
    parts = 2 if channels % 256 == 0 else 1
    share = channels // n
    shares = (n, share, span)
    high, low, inverse = (jnp.asarray(t) for t in fourier_tables(span))
    exps = jnp.transpose(scale_exp, (0, 2, 1))
    reach_row = reach.reshape(1, channels)
    skip_row = skip.reshape(1, channels)
    vmem = pl.BlockSpec(memory_space=pltpu.VMEM)
    hbm = pl.BlockSpec(memory_space=pltpu.HBM)
    remote = pl.BlockSpec(memory_space=pl.ANY)

    def shape(dims, dtype):
        return jax.ShapeDtypeStruct(dims, dtype)

    def call(kernel, name, ins, outs, mib=32, **options):
        return pl.pallas_call(
            kernel,
            in_specs=ins,
            out_specs=[vmem] * len(outs),
            out_shape=outs,
            compiler_params=params(mib),
            name=name,
            **options,
        )

    def swap(value, axis, k):
        return lax.ppermute(value, axis, [(j, j ^ k) for j in range(lax.axis_size(axis))])

    flat = shape((channels, span), BF16)
    part = shape((share, span), BF16)
    line = shape((1, span), F32)
    main, rest, *sends = call(
        functools.partial(prep_kernel, parts, n),
        "prep",
        [hbm] * 3,
        [flat] * (1 + bits),
        mib=53,
        scratch_shapes=[
            pltpu.VMEM((3, channels, span), BF16),
            pltpu.VMEM((3, blocks, channels), jnp.int32),
            pltpu.VMEM((channels, span), BF16),
            pltpu.SemaphoreType.DMA,
            pltpu.SemaphoreType.DMA((parts, 2)),
            pltpu.SemaphoreType.DMA((parts, 2)),
        ],
    )(proj, exps, cotangent)

    sends.append(main)
    first = [swap(sends[k.bit_length() - 1], "ctx", k) for k in range(1, n)]

    def pick(k, *after):
        return call(functools.partial(pick_kernel, k, n), "pick", [vmem] * 2 + [remote] * len(after), [part])(
            main.reshape(shares), rest.reshape(shares), *after
        )[0]

    second = {k: swap(pick(k), "ctx", k) for k in range(2, n)}

    wide = shape((channels, 2 * span), BF16)
    query, base, *wins = call(
        functools.partial(windows_kernel, n, rows),
        "windows",
        [vmem] * 10,
        [flat, shape((2, channels, 2 * span), F32)] + [wide] * (n - 2),
        scratch_shapes=[
            pltpu.VMEM((n + 1, rows, span), BF16),
            pltpu.VMEM((channels, 1), jnp.int32),
            pltpu.VMEM((channels, 1), F32),
        ],
    )(proj, exps, filt, reach_row, skip_row, main, rest, high, low, first[0])
    second[1] = swap(pick(1, first[0]), "ctx", 1)

    acc, response, conv, peak = call(
        functools.partial(conv_kernel, n, seq_len, rows),
        "conv",
        [vmem] * (2 * n),
        [shape((2, channels, 2 * span), F32)] + [shape((channels, span), F32)] * 2 + [line],
        input_output_aliases={2 * n - 4: 0},
    )(*first[1:], *wins, base, query, high, inverse)

    far = swap(peak, "ch", 1)
    own_part, *parts_out, peak = call(
        functools.partial(taps_kernel, n, seq_len),
        "taps",
        [vmem] * (2 * n + 4),
        [part] * n + [line],
        scratch_shapes=[
            pltpu.VMEM(shares, BF16),
            pltpu.VMEM((n + 1, share, span), BF16),
            pltpu.VMEM((n, share, 2 * span), F32),
            pltpu.VMEM((n, share, 2 * span), F32),
            pltpu.VMEM((share, 2 * span), F32),
        ],
    )(
        main.reshape(shares), rest.reshape(shares), reach.reshape(n, 1, share), high, inverse,
        *[x.reshape(shares) for x in first], *[second[k] for k in range(1, n)], peak,
    )
    hop = 2
    while hop < ch_count:
        peak = jnp.maximum(peak, far)
        far = swap(peak, "ch", hop)
        hop *= 2
    scaled_out, peak = call(scale_kernel, "scale", [vmem] * 3, [flat, line])(response, peak, far)

    (gradients,) = call(
        functools.partial(grad_kernel, seq_len, rows),
        "grads",
        [vmem] * 6,
        [shape((3, channels, span), BF16)],
        cost_estimate=pl.CostEstimate(flops=10**9, bytes_accessed=10**6, transcendentals=0),
    )(proj, exps, cotangent, conv, acc, inverse)

    parts_out = [swap(x, "ctx", k + 1) for k, x in enumerate(parts_out)]
    (filter_grad,) = call(functools.partial(spread_kernel, n), "spread", [vmem] * n, [shape(shares, F32)])(
        own_part, *parts_out
    )
    return (scaled_out, peak.reshape(span), gradients, filter_grad.reshape(channels, span))


def solution(mesh):
    return jax.shard_map(
        body,
        mesh=mesh,
        in_specs=(
            P(None, "ch", "ctx"),
            P(None, "ch", "ctx"),
            P("ch", None),
            P("ch"),
            P("ch"),
            P("ch", "ctx"),
        ),
        out_specs=(P("ch", "ctx"), P("ctx"), P(None, "ch", "ctx"), P("ch", "ctx")),
        check_vma=False,
    )
```

```python
import functools
import math

import jax
import jax.numpy as jnp
import ml_dtypes
import numpy as np
from jax import lax
from jax.experimental import pallas as pl
from jax.experimental.pallas import tpu as pltpu
from jax.sharding import PartitionSpec as P

REACH_DIVISORS = (64, 32, 16, 4, 1)
LOAD_MIB = 53.3


def cost(flops):
    return pl.CostEstimate(flops=flops, bytes_accessed=10**6, transcendentals=0)


COSTS = {"load": cost(10**9), "grads": cost(10**9), "scale": cost(10**9)}
F32 = jnp.float32
BF16 = jnp.bfloat16


def fourier_tables(span):
    freq = np.arange(span)
    time = np.arange(2 * span)
    phase = ((2 * freq[None, :] + 1) * time[:, None]) % (4 * span)
    angle = phase * (math.pi / (2 * span))
    forward = np.concatenate([np.cos(angle), -np.sin(angle)], axis=1)
    high = forward.astype(ml_dtypes.bfloat16)
    low = (forward - high.astype(np.float64)).astype(ml_dtypes.bfloat16)
    inverse = (forward.T / span).astype(ml_dtypes.bfloat16)
    return high, low, inverse


def mm(left, right):
    return lax.dot_general(left, right, (((1,), (0,)), ((), ())), preferred_element_type=F32)


def mm2(left, high, low):
    return mm(left, high) + mm(left, low)


def block_scale(exps, span):
    blocks = exps.shape[0]
    block_len = span // blocks
    col = lax.broadcasted_iota(jnp.int32, (blocks, span), 1)
    row = lax.broadcasted_iota(jnp.int32, (blocks, span), 0)
    onehot = jnp.where(col // block_len == row, 1.0, 0.0).astype(BF16)
    scale = jnp.exp2(exps.astype(F32)).astype(BF16)
    return lax.dot_general(scale, onehot, (((0,), (0,)), ((), ())), preferred_element_type=F32)


def column(row_ref):
    row = row_ref[...]
    return jnp.transpose(jnp.broadcast_to(row, (8, row.shape[1])))[:, 0:1]


def reach_lens(reach_ref, seq_len):
    cls = column(reach_ref)
    out = jnp.zeros_like(cls)
    for index, div in enumerate(REACH_DIVISORS):
        out = jnp.where(cls == index, seq_len // div, out)
    return out


def cmul_parts(first, second, half):
    ar, ai = first[:, :half], first[:, half:]
    br, bi = second[:, :half], second[:, half:]
    return ar, ai, br, bi


def row_loop(total, step):
    def run(step_fn):
        if total <= step:
            step_fn(slice(0, total))
            return

        def one(i, carry):
            step_fn(pl.ds(pl.multiple_of(i * step, step), step))
            return carry

        lax.fori_loop(0, total // step, one, 0)

    return run


def top_bit(n):
    return lax.div(lax.axis_index("ctx"), (n + 1) // 2)


def load_kernel(parts, proj_hbm, cot_hbm, key_value_ref, query_cot_ref, proj, cot, key_sem, query_sem):
    channels, span = cot.shape
    rows = channels // parts
    copies = []
    for part in range(parts):
        block = pl.ds(part * rows, rows)
        copies.append(
            (
                pltpu.make_async_copy(proj_hbm.at[pl.ds(1, 2), block], proj.at[pl.ds(1, 2), block], key_sem.at[part]),
                pltpu.make_async_copy(proj_hbm.at[0, block], proj.at[0, block], query_sem.at[part, 0]),
                pltpu.make_async_copy(cot_hbm.at[block], cot.at[block], query_sem.at[part, 1]),
            )
        )
        for copy in copies[-1]:
            copy.start()
    for part in range(parts):
        block = pl.ds(part * rows, rows)
        copies[part][0].wait()
        key_value_ref[block] = (proj[1, block].astype(F32) * proj[2, block].astype(F32)).astype(BF16)
        copies[part][1].wait()
        copies[part][2].wait()
        query_cot_ref[block] = (cot[block].astype(F32) * proj[0, block].astype(F32)).astype(BF16)


def prep_kernel(n, rows, key_value_ref, query_cot_ref, exp_ref, main_ref, rest_ref, *send_refs):
    me = lax.axis_index("ctx")
    upper = top_bit(n)
    channels, span = main_ref.shape
    lows = [lax.rem(lax.div(me, 2**bit), 2) for bit in range(len(send_refs))]
    for first in range(0, channels, rows):
        block = slice(first, first + rows)
        mixed = (
            key_value_ref[block].astype(F32) * block_scale(exp_ref[1, :, block] + exp_ref[2, :, block], span)
        ).astype(BF16)
        pulled = (query_cot_ref[block].astype(F32) * block_scale(exp_ref[0, :, block], span)).astype(BF16)
        for ref, later in [(main_ref, upper), (rest_ref, 1 - upper), *zip(send_refs, lows)]:
            ref[block] = jnp.where(later == 1, pulled, mixed)


def windows_kernel(
    n, rows, proj_ref, exp_ref, filt_ref, reach_ref, skip_ref, main_ref, rest_ref, high_ref, low_ref,
    recv_ref, query_ref, base_ref, *rest
):
    win_refs, (taps, lens, gain) = rest[: n - 2], rest[n - 2 :]
    me = lax.axis_index("ctx")
    channels, seq_len = filt_ref.shape
    span = seq_len // n
    fscale = 1.0 / math.sqrt(seq_len)
    query_ref[...] = (proj_ref[0].astype(F32) * block_scale(exp_ref[0], span)).astype(BF16)
    upper = top_bit(n)
    lens[...] = reach_lens(reach_ref, seq_len)
    gain[...] = column(skip_ref) * (1.0 / fscale)

    @row_loop(channels, rows)
    def _(block):
        count = min(rows, channels)
        taps[0] = jnp.zeros((count, span), BF16)
        for b in range(n):
            lag = lax.broadcasted_iota(jnp.int32, (count, span), 1) + b * span
            taps[b + 1] = jnp.where(
                lag < lens[block], filt_ref[block, b * span : (b + 1) * span].astype(F32), 0.0
            ).astype(BF16)
        near = mm2(taps[1], high_ref[span:], low_ref[span:])
        near += gain[block] * high_ref[span : span + 1, :].astype(F32)
        wr, wi = near[:, :span], near[:, span:]
        for ref, later in ((main_ref, upper), (rest_ref, 1 - upper)):
            start = pl.multiple_of(later * span, span)
            spec = mm2(ref[block], high_ref[pl.ds(start, span), :], low_ref[pl.ds(start, span), :])
            xr, xi = spec[:, :span], spec[:, span:]
            turned = wi * (1 - 2 * later).astype(F32)
            base_ref[later, block, :span] = xr * wr - xi * turned
            base_ref[later, block, span:] = xr * turned + xi * wr
        for k in range(1, n):
            other = jnp.bitwise_xor(me, k)
            dist = jnp.abs(other - me)
            win = mm2(taps[dist], high_ref[:span], low_ref[:span]) + mm2(
                taps[dist + 1], high_ref[span:], low_ref[span:]
            )
            sign = jnp.where(other < me, 1.0, -1.0).astype(F32)
            wr, wi = win[:, :span], win[:, span:] * sign
            if k > 1:
                win_refs[k - 2][block, :span] = wr.astype(BF16)
                win_refs[k - 2][block, span:] = wi.astype(BF16)
                continue
            later = jnp.where(other > me, 1, 0)
            start = pl.multiple_of(later * span, span)
            spec = mm2(recv_ref[block], high_ref[pl.ds(start, span), :], low_ref[pl.ds(start, span), :])
            xr, xi = spec[:, :span], spec[:, span:]
            base_ref[later, block, :span] += xr * wr - xi * wi
            base_ref[later, block, span:] += xr * wi + xi * wr


def conv_kernel(n, seq_len, rows, *refs):
    recv_refs, win_refs = refs[: n - 2], refs[n - 2 : 2 * n - 4]
    _, query_ref, high_ref, inv_ref = refs[2 * n - 4 : 2 * n]
    acc, resp_ref, conv_ref, peak_ref = refs[2 * n :]
    me = lax.axis_index("ctx")
    channels, span = query_ref.shape
    fscale = 1.0 / math.sqrt(seq_len)
    peak_ref[...] = jnp.zeros_like(peak_ref)

    @row_loop(channels, rows)
    def _(block):
        for k in range(2, n):
            later = jnp.where(jnp.bitwise_xor(me, k) > me, 1, 0)
            start = pl.multiple_of(later * span, span)
            spec = mm(recv_refs[k - 2][block], high_ref[pl.ds(start, span), :])
            xr, xi = spec[:, :span], spec[:, span:]
            wr = win_refs[k - 2][block, :span].astype(F32)
            wi = win_refs[k - 2][block, span:].astype(F32)
            acc[later, block, :span] += xr * wr - xi * wi
            acc[later, block, span:] += xr * wi + xi * wr
        conv = mm(acc[0, block].astype(BF16), inv_ref[:, span:]) * fscale
        response = query_ref[block].astype(F32) * conv
        resp_ref[block] = response
        conv_ref[block] = conv
        peak_ref[...] = jnp.maximum(peak_ref[...], jnp.max(jnp.abs(response), axis=0, keepdims=True))


def taps_kernel(n, seq_len, main_ref, rest_ref, reach_ref, high_ref, inv_ref, *refs):
    first_refs, second_refs, refs = refs[: n - 1], refs[n - 1 : 2 * n - 2], refs[2 * n - 2 :]
    peak_ref, out_refs, top_ref = refs[0], refs[1 : n + 1], refs[n + 1]
    mbuf, pbuf, mspec, pspec, acc, out = refs[n + 2 :]
    top_ref[...] = peak_ref[...]
    me = lax.axis_index("ctx")
    _, rows, span = mbuf.shape
    fscale = 1.0 / math.sqrt(seq_len)
    upper = top_bit(n)

    @pl.when(upper == 0)
    def _():
        mbuf[me] = main_ref[me]
        pbuf[me] = rest_ref[me]

    @pl.when(upper == 1)
    def _():
        mbuf[me] = rest_ref[me]
        pbuf[me] = main_ref[me]

    pbuf[n] = jnp.zeros((rows, span), BF16)
    for k in range(1, n):
        other = jnp.bitwise_xor(me, k)

        @pl.when(other < me)
        def _():
            mbuf[other] = first_refs[k - 1][me]
            pbuf[other] = second_refs[k - 1][...]

        @pl.when(other > me)
        def _():
            pbuf[other] = first_refs[k - 1][me]
            mbuf[other] = second_refs[k - 1][...]

    if rows % 16 == 0:
        flat = (n * rows, span)
        mspec[...] = mm(mbuf[...].reshape(flat), high_ref[:span]).reshape(mspec.shape)
        pair = jnp.concatenate([pbuf[:n].reshape(flat), pbuf[1:].reshape(flat)], axis=1)
        pspec[...] = mm(pair, high_ref[...]).reshape(pspec.shape)
    else:
        for b in range(n):
            mspec[b] = mm(mbuf[b], high_ref[:span])
            pspec[b] = mm(pbuf[b], high_ref[:span]) + mm(pbuf[b + 1], high_ref[span:])

    @row_loop(rows, 16)
    def _(tile):
        for lag_block in range(n):
            real = imag = 0.0
            for b in range(n - lag_block):
                ar, ai = mspec[b, tile, :span], mspec[b, tile, span:]
                br, bi = pspec[b + lag_block, tile, :span], pspec[b + lag_block, tile, span:]
                real += ar * br + ai * bi
                imag += ar * bi - ai * br
            acc[lag_block, tile, :span] = real.astype(BF16)
            acc[lag_block, tile, span:] = imag.astype(BF16)

    lens = reach_lens(reach_ref.at[me], seq_len)
    for lag_block in range(n):
        lag = lax.broadcasted_iota(jnp.int32, (rows, span), 1) + lag_block * span
        own = mm(acc[lag_block], inv_ref[:, :span]) * fscale
        out[lag_block] = jnp.where(lag < lens, own, 0.0).astype(BF16)
    for k in range(n):
        out_refs[k][...] = out[jnp.bitwise_xor(me, k)]


def pick_kernel(k, n, main_ref, rest_ref, *refs):
    me = lax.axis_index("ctx")
    other = jnp.bitwise_xor(me, k)
    out_ref = refs[-1]

    wanted = jnp.where(other > me, 1, 0)

    @pl.when(wanted == top_bit(n))
    def _():
        out_ref[...] = main_ref[other]

    @pl.when(wanted != top_bit(n))
    def _():
        out_ref[...] = rest_ref[other]


def grads_kernel(seq_len, proj_ref, exp_ref, cot_ref, conv_ref, acc_ref, inv_ref, *refs):
    grad_hbm, grad, grad_sem = refs
    span = cot_ref.shape[1]
    fscale = 1.0 / math.sqrt(seq_len)
    copies = []

    def send(source, target, sem):
        copies.append(pltpu.make_async_copy(source, target, sem))
        copies[-1].start()

    grad[0] = (cot_ref[...].astype(F32) * conv_ref[...]).astype(BF16)
    send(grad.at[0], grad_hbm.at[0], grad_sem.at[0])
    grad_mixed = mm(acc_ref[1].astype(BF16), inv_ref[:, :span]) * fscale
    for slot, source in ((1, 2), (2, 1)):
        scaled = proj_ref[source].astype(F32) * block_scale(exp_ref[source], span)
        grad[slot] = (grad_mixed * scaled).astype(BF16)
        send(grad.at[slot], grad_hbm.at[slot], grad_sem.at[slot])
    for copy in copies:
        copy.wait()


def spread_kernel(n, *refs):
    part_refs, (near_ref, taps_hbm, peak_ref, taps, taps_sem) = refs[:n], refs[n:]
    me = lax.axis_index("ctx")
    peak_ref[...] = near_ref[...]
    copies = []
    for k in range(n):
        block = jnp.bitwise_xor(me, k)
        taps[block] = part_refs[k][...].astype(F32)
        copies.append(pltpu.make_async_copy(taps.at[block], taps_hbm.at[block], taps_sem.at[k]))
        copies[-1].start()
    for copy in copies:
        copy.wait()


def scale_kernel(resp_ref, near_ref, far_ref, out_ref, peak_ref):
    peak = jnp.maximum(near_ref[...], far_ref[...])
    peak_ref[...] = peak
    out_ref[...] = (resp_ref[...] * (1.0 / (peak + 1e-06))).astype(BF16)


def params(mib=32):
    return pltpu.CompilerParams(vmem_limit_bytes=int(mib * 2**20))


def body(proj, scale_exp, filt, reach, skip, cotangent):
    groups, channels, span = proj.shape
    n = lax.axis_size("ctx")
    ch_count = lax.axis_size("ch")
    seq_len = n * span
    blocks = scale_exp.shape[2]
    bits = max(1, (n - 1).bit_length())
    rows = channels
    parts = 2 if channels % 256 == 0 else 1
    share = channels // n
    shares = (n, share, span)
    high, low, inverse = (jnp.asarray(t) for t in fourier_tables(span))
    exps = jnp.transpose(scale_exp, (0, 2, 1))
    reach_row = reach.reshape(1, channels)
    skip_row = skip.reshape(1, channels)
    vmem = pl.BlockSpec(memory_space=pltpu.VMEM)
    hbm = pl.BlockSpec(memory_space=pltpu.HBM)
    remote = pl.BlockSpec(memory_space=pl.ANY)

    def shape(dims, dtype):
        return jax.ShapeDtypeStruct(dims, dtype)

    def call(kernel, name, ins, outs, mib=32, out_specs=None, **options):
        return pl.pallas_call(
            kernel,
            in_specs=ins,
            out_specs=out_specs or [vmem] * len(outs),
            out_shape=outs,
            compiler_params=params(mib),
            name=name,
            cost_estimate=COSTS.get(name),
            **options,
        )

    def swap(value, axis, k):
        return lax.ppermute(value, axis, [(j, j ^ k) for j in range(lax.axis_size(axis))])

    flat = shape((channels, span), BF16)
    part = shape((share, span), BF16)
    line = shape((1, span), F32)
    raw = call(
        functools.partial(load_kernel, parts),
        "load",
        [hbm] * 2,
        [flat] * 2,
        mib=LOAD_MIB,
        scratch_shapes=[
            pltpu.VMEM((3, channels, span), BF16),
            pltpu.VMEM((channels, span), BF16),
            pltpu.SemaphoreType.DMA((parts,)),
            pltpu.SemaphoreType.DMA((parts, 2)),
        ],
    )(proj, cotangent)
    main, rest, *sends = call(
        functools.partial(prep_kernel, n, rows), "prep", [vmem] * 3, [flat] * (1 + bits)
    )(*raw, exps)
    sends.append(main)
    first = [swap(sends[k.bit_length() - 1], "ctx", k) for k in range(1, n)]

    def pick(k, *after):
        return call(functools.partial(pick_kernel, k, n), "pick", [vmem] * 2 + [remote] * len(after), [part])(
            main.reshape(shares), rest.reshape(shares), *after
        )[0]

    second = {k: swap(pick(k), "ctx", k) for k in range(2, n)}

    wide = shape((channels, 2 * span), BF16)
    query, base, *wins = call(
        functools.partial(windows_kernel, n, rows),
        "windows",
        [vmem] * 10,
        [flat, shape((2, channels, 2 * span), F32)] + [wide] * (n - 2),
        scratch_shapes=[
            pltpu.VMEM((n + 1, rows, span), BF16),
            pltpu.VMEM((channels, 1), jnp.int32),
            pltpu.VMEM((channels, 1), F32),
        ],
    )(proj, exps, filt, reach_row, skip_row, main, rest, high, low, first[0])
    second[1] = swap(pick(1, first[0]), "ctx", 1)

    acc, response, conv, peak = call(
        functools.partial(conv_kernel, n, seq_len, rows),
        "conv",
        [vmem] * (2 * n),
        [shape((2, channels, 2 * span), F32)] + [shape((channels, span), F32)] * 2 + [line],
        input_output_aliases={2 * n - 4: 0},
    )(*first[1:], *wins, base, query, high, inverse)

    far = swap(peak, "ch", 1)
    own_part, *parts_out, peak = call(
        functools.partial(taps_kernel, n, seq_len),
        "taps",
        [vmem] * (2 * n + 4),
        [part] * n + [line],
        scratch_shapes=[
            pltpu.VMEM(shares, BF16),
            pltpu.VMEM((n + 1, share, span), BF16),
            pltpu.VMEM((n, share, 2 * span), F32),
            pltpu.VMEM((n, share, 2 * span), F32),
            pltpu.VMEM((n, share, 2 * span), BF16),
            pltpu.VMEM(shares, BF16),
        ],
    )(
        main.reshape(shares), rest.reshape(shares), reach.reshape(n, 1, share), high, inverse,
        *[x.reshape(shares) for x in first], *[second[k] for k in range(1, n)], peak,
    )
    hop = 2
    while hop < ch_count:
        peak = jnp.maximum(peak, far)
        far = swap(peak, "ch", hop)
        hop *= 2
    parts_out = [swap(x, "ctx", k + 1) for k, x in enumerate(parts_out)]
    (gradients,) = call(
        functools.partial(grads_kernel, seq_len),
        "grads",
        [vmem] * 6,
        [shape((3, channels, span), BF16)],
        out_specs=[hbm],
        scratch_shapes=[pltpu.VMEM((3, channels, span), BF16), pltpu.SemaphoreType.DMA((3,))],
    )(proj, exps, cotangent, conv, acc, inverse)
    filter_grad, peak = call(
        functools.partial(spread_kernel, n),
        "spread",
        [vmem] * (n + 1),
        [shape(shares, F32), line],
        out_specs=[hbm, vmem],
        scratch_shapes=[pltpu.VMEM(shares, F32), pltpu.SemaphoreType.DMA((n,))],
    )(own_part, *parts_out, peak)
    scaled_out, peak = call(scale_kernel, "scale", [vmem] * 3, [flat, line])(response, peak, far)
    return (scaled_out, peak.reshape(span), gradients, filter_grad.reshape(channels, span))


def solution(mesh):
    return jax.shard_map(
        body,
        mesh=mesh,
        in_specs=(
            P(None, "ch", "ctx"),
            P(None, "ch", "ctx"),
            P("ch", None),
            P("ch"),
            P("ch"),
            P("ch", "ctx"),
        ),
        out_specs=(P("ch", "ctx"), P("ctx"), P(None, "ch", "ctx"), P("ch", "ctx")),
        check_vma=False,
    )
```

```python
import functools
import math

import jax
import jax.numpy as jnp
import ml_dtypes
import numpy as np
from jax import lax
from jax.experimental import pallas as pl
from jax.experimental.pallas import tpu as pltpu
from jax.sharding import PartitionSpec as P

REACH_DIVISORS = (64, 32, 16, 4, 1)
LOAD_MIB = 53.3


def cost(flops):
    return pl.CostEstimate(flops=flops, bytes_accessed=10**6, transcendentals=0)


COSTS = {"load": cost(10**9), "grads": cost(10**9), "scale": cost(10**9)}
F32 = jnp.float32
BF16 = jnp.bfloat16


def fourier_tables(span):
    freq = np.arange(span)
    time = np.arange(2 * span)
    phase = ((2 * freq[None, :] + 1) * time[:, None]) % (4 * span)
    angle = phase * (math.pi / (2 * span))
    forward = np.concatenate([np.cos(angle), -np.sin(angle)], axis=1)
    high = forward.astype(ml_dtypes.bfloat16)
    low = (forward - high.astype(np.float64)).astype(ml_dtypes.bfloat16)
    inverse = (forward.T / span).astype(ml_dtypes.bfloat16)
    return high, low, inverse


def mm(left, right):
    return lax.dot_general(left, right, (((1,), (0,)), ((), ())), preferred_element_type=F32)


def mm2(left, high, low):
    return mm(left, high) + mm(left, low)


def block_scale(exps, span):
    blocks = exps.shape[0]
    block_len = span // blocks
    col = lax.broadcasted_iota(jnp.int32, (blocks, span), 1)
    row = lax.broadcasted_iota(jnp.int32, (blocks, span), 0)
    onehot = jnp.where(col // block_len == row, 1.0, 0.0).astype(BF16)
    scale = jnp.exp2(exps.astype(F32)).astype(BF16)
    return lax.dot_general(scale, onehot, (((0,), (0,)), ((), ())), preferred_element_type=F32)


def column(row_ref):
    row = row_ref[...]
    return jnp.transpose(jnp.broadcast_to(row, (8, row.shape[1])))[:, 0:1]


def reach_lens(reach_ref, seq_len):
    cls = column(reach_ref)
    out = jnp.zeros_like(cls)
    for index, div in enumerate(REACH_DIVISORS):
        out = jnp.where(cls == index, seq_len // div, out)
    return out


def cmul_parts(first, second, half):
    ar, ai = first[:, :half], first[:, half:]
    br, bi = second[:, :half], second[:, half:]
    return ar, ai, br, bi


def row_loop(total, step):
    def run(step_fn):
        if total <= step:
            step_fn(slice(0, total))
            return

        def one(i, carry):
            step_fn(pl.ds(pl.multiple_of(i * step, step), step))
            return carry

        lax.fori_loop(0, total // step, one, 0)

    return run


def top_bit(n):
    return lax.div(lax.axis_index("ctx"), (n + 1) // 2)


def load_kernel(parts, proj_hbm, cot_hbm, key_value_ref, query_cot_ref, proj, cot, key_sem, query_sem):
    channels, span = cot.shape
    rows = channels // parts
    copies = []
    for part in range(parts):
        block = pl.ds(part * rows, rows)
        copies.append(
            (
                pltpu.make_async_copy(proj_hbm.at[pl.ds(1, 2), block], proj.at[pl.ds(1, 2), block], key_sem.at[part]),
                pltpu.make_async_copy(proj_hbm.at[0, block], proj.at[0, block], query_sem.at[part, 0]),
                pltpu.make_async_copy(cot_hbm.at[block], cot.at[block], query_sem.at[part, 1]),
            )
        )
        for copy in copies[-1]:
            copy.start()
    for part in range(parts):
        block = pl.ds(part * rows, rows)
        copies[part][0].wait()
        key_value_ref[block] = (proj[1, block].astype(F32) * proj[2, block].astype(F32)).astype(BF16)
        copies[part][1].wait()
        copies[part][2].wait()
        query_cot_ref[block] = (cot[block].astype(F32) * proj[0, block].astype(F32)).astype(BF16)


def prep_kernel(n, rows, key_value_ref, query_cot_ref, exp_ref, main_ref, rest_ref, *send_refs):
    me = lax.axis_index("ctx")
    upper = top_bit(n)
    channels, span = main_ref.shape
    lows = [lax.rem(lax.div(me, 2**bit), 2) for bit in range(len(send_refs))]
    for first in range(0, channels, rows):
        block = slice(first, first + rows)
        mixed = (
            key_value_ref[block].astype(F32) * block_scale(exp_ref[1, :, block] + exp_ref[2, :, block], span)
        ).astype(BF16)
        pulled = (query_cot_ref[block].astype(F32) * block_scale(exp_ref[0, :, block], span)).astype(BF16)
        for ref, later in [(main_ref, upper), (rest_ref, 1 - upper), *zip(send_refs, lows)]:
            ref[block] = jnp.where(later == 1, pulled, mixed)


def windows_kernel(
    n, rows, proj_ref, exp_ref, filt_ref, reach_ref, skip_ref, main_ref, rest_ref, high_ref, low_ref,
    recv_ref, deq_ref, base_ref, *rest
):
    win_refs, (taps, lens, gain) = rest[: n - 2], rest[n - 2 :]
    me = lax.axis_index("ctx")
    channels, seq_len = filt_ref.shape
    span = seq_len // n
    fscale = 1.0 / math.sqrt(seq_len)
    for group in range(3):
        deq_ref[group] = (proj_ref[group].astype(F32) * block_scale(exp_ref[group], span)).astype(BF16)
    upper = top_bit(n)
    lens[...] = reach_lens(reach_ref, seq_len)
    gain[...] = column(skip_ref) * (1.0 / fscale)

    @row_loop(channels, rows)
    def _(block):
        count = min(rows, channels)
        taps[0] = jnp.zeros((count, span), BF16)
        for b in range(n):
            lag = lax.broadcasted_iota(jnp.int32, (count, span), 1) + b * span
            taps[b + 1] = jnp.where(
                lag < lens[block], filt_ref[block, b * span : (b + 1) * span].astype(F32), 0.0
            ).astype(BF16)
        near = mm2(taps[1], high_ref[span:], low_ref[span:])
        near += gain[block] * high_ref[span : span + 1, :].astype(F32)
        wr, wi = near[:, :span], near[:, span:]
        for ref, later in ((main_ref, upper), (rest_ref, 1 - upper)):
            start = pl.multiple_of(later * span, span)
            spec = mm2(ref[block], high_ref[pl.ds(start, span), :], low_ref[pl.ds(start, span), :])
            xr, xi = spec[:, :span], spec[:, span:]
            turned = wi * (1 - 2 * later).astype(F32)
            base_ref[later, block, :span] = xr * wr - xi * turned
            base_ref[later, block, span:] = xr * turned + xi * wr
        for k in range(1, n):
            other = jnp.bitwise_xor(me, k)
            dist = jnp.abs(other - me)
            win = mm2(taps[dist], high_ref[:span], low_ref[:span]) + mm2(
                taps[dist + 1], high_ref[span:], low_ref[span:]
            )
            sign = jnp.where(other < me, 1.0, -1.0).astype(F32)
            wr, wi = win[:, :span], win[:, span:] * sign
            if k > 1:
                win_refs[k - 2][block, :span] = wr.astype(BF16)
                win_refs[k - 2][block, span:] = wi.astype(BF16)
                continue
            later = jnp.where(other > me, 1, 0)
            start = pl.multiple_of(later * span, span)
            spec = mm2(recv_ref[block], high_ref[pl.ds(start, span), :], low_ref[pl.ds(start, span), :])
            xr, xi = spec[:, :span], spec[:, span:]
            base_ref[later, block, :span] += xr * wr - xi * wi
            base_ref[later, block, span:] += xr * wi + xi * wr


def conv_kernel(n, seq_len, rows, *refs):
    recv_refs, win_refs, refs = refs[: n - 2], refs[n - 2 : 2 * n - 4], refs[2 * n - 4 :]
    base_ref, deq_ref, high_ref, inv_ref, back_ref, resp_ref, conv_ref, peak_ref = refs
    me = lax.axis_index("ctx")
    channels, span = resp_ref.shape
    fscale = 1.0 / math.sqrt(seq_len)
    uppers = [lax.rem(lax.div(me, 2**bit), 2) for bit in range((n - 1).bit_length())]
    starts = [pl.multiple_of((1 - upper) * span, span) for upper in uppers]
    peaks = []
    for first in range(0, channels, rows):
        tile = slice(first, first + rows)
        fr, fi = base_ref[0, tile, :span], base_ref[0, tile, span:]
        br, bi = base_ref[1, tile, :span], base_ref[1, tile, span:]
        for bit in range(1, len(uppers)):
            real = imag = 0.0
            for k in range(2**bit, min(2 ** (bit + 1), n)):
                spec = mm(recv_refs[k - 2][tile], high_ref[pl.ds(starts[bit], span), :])
                xr, xi = spec[:, :span], spec[:, span:]
                wr = win_refs[k - 2][tile, :span].astype(F32)
                wi = win_refs[k - 2][tile, span:].astype(F32)
                real += xr * wr - xi * wi
                imag += xr * wi + xi * wr
            here = uppers[bit] == 1
            fr, br = jnp.where(here, fr + real, fr), jnp.where(here, br, br + real)
            fi, bi = jnp.where(here, fi + imag, fi), jnp.where(here, bi, bi + imag)
        back_ref[tile, :span], back_ref[tile, span:] = br.astype(BF16), bi.astype(BF16)
        front = jnp.concatenate([fr.astype(BF16), fi.astype(BF16)], axis=1)
        conv = mm(front, inv_ref[:, span:]) * fscale
        response = deq_ref[0, tile].astype(F32) * conv
        resp_ref[tile] = response
        conv_ref[tile] = conv
        peaks.append(jnp.max(jnp.abs(response), axis=0, keepdims=True))
    peak_ref[...] = functools.reduce(jnp.maximum, peaks)


def taps_kernel(n, seq_len, main_ref, rest_ref, reach_ref, high_ref, inv_ref, *refs):
    first_refs, second_refs, refs = refs[: n - 1], refs[n - 1 : 2 * n - 2], refs[2 * n - 2 :]
    peak_ref, out_refs, top_ref = refs[0], refs[1 : n + 1], refs[n + 1]
    mbuf, pbuf, mspec, pspec, acc, out = refs[n + 2 :]
    top_ref[...] = peak_ref[...]
    me = lax.axis_index("ctx")
    _, rows, span = mbuf.shape
    fscale = 1.0 / math.sqrt(seq_len)
    upper = top_bit(n)

    @pl.when(upper == 0)
    def _():
        mbuf[me] = main_ref[me]
        pbuf[me] = rest_ref[me]

    @pl.when(upper == 1)
    def _():
        mbuf[me] = rest_ref[me]
        pbuf[me] = main_ref[me]

    pbuf[n] = jnp.zeros((rows, span), BF16)
    for k in range(1, n):
        other = jnp.bitwise_xor(me, k)

        @pl.when(other < me)
        def _():
            mbuf[other] = first_refs[k - 1][me]
            pbuf[other] = second_refs[k - 1][...]

        @pl.when(other > me)
        def _():
            pbuf[other] = first_refs[k - 1][me]
            mbuf[other] = second_refs[k - 1][...]

    if rows % 16 == 0:
        flat = (n * rows, span)
        mspec[...] = mm(mbuf[...].reshape(flat), high_ref[:span]).reshape(mspec.shape)
        pair = jnp.concatenate([pbuf[:n].reshape(flat), pbuf[1:].reshape(flat)], axis=1)
        pspec[...] = mm(pair, high_ref[...]).reshape(pspec.shape)
    else:
        for b in range(n):
            mspec[b] = mm(mbuf[b], high_ref[:span])
            pspec[b] = mm(pbuf[b], high_ref[:span]) + mm(pbuf[b + 1], high_ref[span:])

    @row_loop(rows, rows)
    def _(tile):
        for lag_block in range(n):
            real = imag = 0.0
            for b in range(n - lag_block):
                ar, ai = mspec[b, tile, :span], mspec[b, tile, span:]
                br, bi = pspec[b + lag_block, tile, :span], pspec[b + lag_block, tile, span:]
                real += ar * br + ai * bi
                imag += ar * bi - ai * br
            acc[lag_block, tile, :span] = real.astype(BF16)
            acc[lag_block, tile, span:] = imag.astype(BF16)

    lens = reach_lens(reach_ref.at[me], seq_len)
    for lag_block in range(n):
        lag = lax.broadcasted_iota(jnp.int32, (rows, span), 1) + lag_block * span
        own = mm(acc[lag_block], inv_ref[:, :span]) * fscale
        out[lag_block] = jnp.where(lag < lens, own, 0.0).astype(BF16)
    for k in range(n):
        out_refs[k][...] = out[jnp.bitwise_xor(me, k)]


def pick_kernel(k, n, main_ref, rest_ref, *refs):
    me = lax.axis_index("ctx")
    other = jnp.bitwise_xor(me, k)
    out_ref = refs[-1]

    wanted = jnp.where(other > me, 1, 0)

    @pl.when(wanted == top_bit(n))
    def _():
        out_ref[...] = main_ref[other]

    @pl.when(wanted != top_bit(n))
    def _():
        out_ref[...] = rest_ref[other]


def grads_kernel(seq_len, deq_ref, cot_ref, conv_ref, back_ref, inv_ref, grad_hbm, grad, grad_sem):
    span = cot_ref.shape[1]
    fscale = 1.0 / math.sqrt(seq_len)
    copies = []

    def send(slot, value):
        grad[slot] = value.astype(BF16)
        copies.append(pltpu.make_async_copy(grad.at[slot], grad_hbm.at[slot], grad_sem.at[slot]))
        copies[-1].start()

    send(0, cot_ref[...].astype(F32) * conv_ref[...])
    grad_mixed = mm(back_ref[...], inv_ref[:, :span]) * fscale
    send(1, grad_mixed * deq_ref[2].astype(F32))
    send(2, grad_mixed * deq_ref[1].astype(F32))
    for copy in copies:
        copy.wait()


def spread_kernel(n, *refs):
    part_refs, (near_ref, taps_hbm, peak_ref, taps, taps_sem) = refs[:n], refs[n:]
    me = lax.axis_index("ctx")
    peak_ref[...] = near_ref[...]
    copies = []
    for k in range(n):
        block = jnp.bitwise_xor(me, k)
        taps[block] = part_refs[k][...].astype(F32)
        copies.append(pltpu.make_async_copy(taps.at[block], taps_hbm.at[block], taps_sem.at[k]))
        copies[-1].start()
    for copy in copies:
        copy.wait()


def scale_kernel(resp_ref, near_ref, far_ref, out_ref, peak_ref):
    peak = jnp.maximum(near_ref[...], far_ref[...])
    peak_ref[...] = peak
    out_ref[...] = (resp_ref[...] * (1.0 / (peak + 1e-06))).astype(BF16)


def params(mib=32):
    return pltpu.CompilerParams(vmem_limit_bytes=int(mib * 2**20))


def body(proj, scale_exp, filt, reach, skip, cotangent):
    groups, channels, span = proj.shape
    n = lax.axis_size("ctx")
    ch_count = lax.axis_size("ch")
    seq_len = n * span
    blocks = scale_exp.shape[2]
    bits = max(1, (n - 1).bit_length())
    rows = channels
    parts = 2 if channels % 256 == 0 else 1
    share = channels // n
    shares = (n, share, span)
    high, low, inverse = (jnp.asarray(t) for t in fourier_tables(span))
    exps = jnp.transpose(scale_exp, (0, 2, 1))
    reach_row = reach.reshape(1, channels)
    skip_row = skip.reshape(1, channels)
    vmem = pl.BlockSpec(memory_space=pltpu.VMEM)
    hbm = pl.BlockSpec(memory_space=pltpu.HBM)
    remote = pl.BlockSpec(memory_space=pl.ANY)

    def shape(dims, dtype):
        return jax.ShapeDtypeStruct(dims, dtype)

    def call(kernel, name, ins, outs, mib=32, out_specs=None, **options):
        return pl.pallas_call(
            kernel,
            in_specs=ins,
            out_specs=out_specs or [vmem] * len(outs),
            out_shape=outs,
            compiler_params=params(mib),
            name=name,
            cost_estimate=COSTS.get(name),
            **options,
        )

    def swap(value, axis, k):
        return lax.ppermute(value, axis, [(j, j ^ k) for j in range(lax.axis_size(axis))])

    flat = shape((channels, span), BF16)
    part = shape((share, span), BF16)
    line = shape((1, span), F32)
    raw = call(
        functools.partial(load_kernel, parts),
        "load",
        [hbm] * 2,
        [flat] * 2,
        mib=LOAD_MIB,
        scratch_shapes=[
            pltpu.VMEM((3, channels, span), BF16),
            pltpu.VMEM((channels, span), BF16),
            pltpu.SemaphoreType.DMA((parts,)),
            pltpu.SemaphoreType.DMA((parts, 2)),
        ],
    )(proj, cotangent)
    main, rest, *sends = call(
        functools.partial(prep_kernel, n, rows), "prep", [vmem] * 3, [flat] * (1 + bits)
    )(*raw, exps)
    sends.append(main)
    first = [swap(sends[k.bit_length() - 1], "ctx", k) for k in range(1, n)]

    def pick(k, *after):
        return call(functools.partial(pick_kernel, k, n), "pick", [vmem] * 2 + [remote] * len(after), [part])(
            main.reshape(shares), rest.reshape(shares), *after
        )[0]

    second = {k: swap(pick(k), "ctx", k) for k in range(2, n)}

    wide = shape((channels, 2 * span), BF16)
    deq, base, *wins = call(
        functools.partial(windows_kernel, n, rows),
        "windows",
        [vmem] * 10,
        [shape((3, channels, span), BF16), shape((2, channels, 2 * span), F32)] + [wide] * (n - 2),
        scratch_shapes=[
            pltpu.VMEM((n + 1, rows, span), BF16),
            pltpu.VMEM((channels, 1), jnp.int32),
            pltpu.VMEM((channels, 1), F32),
        ],
    )(proj, exps, filt, reach_row, skip_row, main, rest, high, low, first[0])
    second[1] = swap(pick(1, first[0]), "ctx", 1)

    back, response, conv, peak = call(
        functools.partial(conv_kernel, n, seq_len, channels),
        "conv",
        [vmem] * (2 * n),
        [wide] + [shape((channels, span), F32)] * 2 + [line],
    )(*first[1:], *wins, base, deq, high, inverse)

    far = swap(peak, "ch", 1)
    own_part, *parts_out, peak = call(
        functools.partial(taps_kernel, n, seq_len),
        "taps",
        [vmem] * (2 * n + 4),
        [part] * n + [line],
        scratch_shapes=[
            pltpu.VMEM(shares, BF16),
            pltpu.VMEM((n + 1, share, span), BF16),
            pltpu.VMEM((n, share, 2 * span), F32),
            pltpu.VMEM((n, share, 2 * span), F32),
            pltpu.VMEM((n, share, 2 * span), BF16),
            pltpu.VMEM(shares, BF16),
        ],
    )(
        main.reshape(shares), rest.reshape(shares), reach.reshape(n, 1, share), high, inverse,
        *[x.reshape(shares) for x in first], *[second[k] for k in range(1, n)], peak,
    )
    hop = 2
    while hop < ch_count:
        peak = jnp.maximum(peak, far)
        far = swap(peak, "ch", hop)
        hop *= 2
    parts_out = [swap(x, "ctx", k + 1) for k, x in enumerate(parts_out)]
    (gradients,) = call(
        functools.partial(grads_kernel, seq_len),
        "grads",
        [vmem] * 5,
        [shape((3, channels, span), BF16)],
        out_specs=[hbm],
        scratch_shapes=[pltpu.VMEM((3, channels, span), BF16), pltpu.SemaphoreType.DMA((3,))],
    )(deq, cotangent, conv, back, inverse)
    filter_grad, peak = call(
        functools.partial(spread_kernel, n),
        "spread",
        [vmem] * (n + 1),
        [shape(shares, F32), line],
        out_specs=[hbm, vmem],
        scratch_shapes=[pltpu.VMEM(shares, F32), pltpu.SemaphoreType.DMA((n,))],
    )(own_part, *parts_out, peak)
    scaled_out, peak = call(scale_kernel, "scale", [vmem] * 3, [flat, line])(response, peak, far)
    return (scaled_out, peak.reshape(span), gradients, filter_grad.reshape(channels, span))


def solution(mesh):
    return jax.shard_map(
        body,
        mesh=mesh,
        in_specs=(
            P(None, "ch", "ctx"),
            P(None, "ch", "ctx"),
            P("ch", None),
            P("ch"),
            P("ch"),
            P("ch", "ctx"),
        ),
        out_specs=(P("ch", "ctx"), P("ctx"), P(None, "ch", "ctx"), P("ch", "ctx")),
        check_vma=False,
    )
```

```python
import functools
import math

import jax
import jax.numpy as jnp
import ml_dtypes
import numpy as np
from jax import lax
from jax.experimental import pallas as pl
from jax.experimental.pallas import tpu as pltpu
from jax.sharding import PartitionSpec as P

REACH_DIVISORS = (64, 32, 16, 4, 1)
LOAD_MIB = 53.3


def cost(flops):
    return pl.CostEstimate(flops=flops, bytes_accessed=10**6, transcendentals=0)


COSTS = {"load": cost(10**9), "grads": cost(10**9), "scale": cost(10**9)}
F32 = jnp.float32
BF16 = jnp.bfloat16


def fourier_tables(span):
    freq = np.arange(span)
    time = np.arange(2 * span)
    phase = ((2 * freq[None, :] + 1) * time[:, None]) % (4 * span)
    angle = phase * (math.pi / (2 * span))
    forward = np.concatenate([np.cos(angle), -np.sin(angle)], axis=1)
    high = forward.astype(ml_dtypes.bfloat16)
    low = (forward - high.astype(np.float64)).astype(ml_dtypes.bfloat16)
    inverse = (forward.T / span).astype(ml_dtypes.bfloat16)
    return high, low, inverse


def mm(left, right):
    return lax.dot_general(left, right, (((1,), (0,)), ((), ())), preferred_element_type=F32)


def mm2(left, high, low):
    return mm(left, high) + mm(left, low)


def block_scale(exps, span):
    blocks = exps.shape[0]
    block_len = span // blocks
    col = lax.broadcasted_iota(jnp.int32, (blocks, span), 1)
    row = lax.broadcasted_iota(jnp.int32, (blocks, span), 0)
    onehot = jnp.where(col // block_len == row, 1.0, 0.0).astype(BF16)
    scale = jnp.exp2(exps.astype(F32)).astype(BF16)
    return lax.dot_general(scale, onehot, (((0,), (0,)), ((), ())), preferred_element_type=F32)


def column(row_ref):
    row = row_ref[...]
    return jnp.transpose(jnp.broadcast_to(row, (8, row.shape[1])))[:, 0:1]


def reach_lens(reach_ref, seq_len):
    cls = column(reach_ref)
    out = jnp.zeros_like(cls)
    for index, div in enumerate(REACH_DIVISORS):
        out = jnp.where(cls == index, seq_len // div, out)
    return out


def cmul_parts(first, second, half):
    ar, ai = first[:, :half], first[:, half:]
    br, bi = second[:, :half], second[:, half:]
    return ar, ai, br, bi


def row_loop(total, step):
    def run(step_fn):
        if total <= step:
            step_fn(slice(0, total))
            return

        def one(i, carry):
            step_fn(pl.ds(pl.multiple_of(i * step, step), step))
            return carry

        lax.fori_loop(0, total // step, one, 0)

    return run


def early(n):
    return min(3, n - 1)


def others(n):
    return [k for k in range(1, n) if k != early(n)]


def top_bit(n):
    return lax.div(lax.axis_index("ctx"), (n + 1) // 2)


def load_kernel(parts, proj_hbm, cot_hbm, key_value_ref, query_cot_ref, proj, cot, key_sem, query_sem):
    channels, span = cot.shape
    rows = channels // parts
    copies = []
    for part in range(parts):
        block = pl.ds(part * rows, rows)
        copies.append(
            (
                pltpu.make_async_copy(proj_hbm.at[pl.ds(1, 2), block], proj.at[pl.ds(1, 2), block], key_sem.at[part]),
                pltpu.make_async_copy(proj_hbm.at[0, block], proj.at[0, block], query_sem.at[part, 0]),
                pltpu.make_async_copy(cot_hbm.at[block], cot.at[block], query_sem.at[part, 1]),
            )
        )
        for copy in copies[-1]:
            copy.start()
    for part in range(parts):
        block = pl.ds(part * rows, rows)
        copies[part][0].wait()
        key_value_ref[block] = (proj[1, block].astype(F32) * proj[2, block].astype(F32)).astype(BF16)
        copies[part][1].wait()
        copies[part][2].wait()
        query_cot_ref[block] = (cot[block].astype(F32) * proj[0, block].astype(F32)).astype(BF16)


def prep_kernel(n, rows, key_value_ref, query_cot_ref, exp_ref, main_ref, rest_ref, *send_refs):
    me = lax.axis_index("ctx")
    upper = top_bit(n)
    channels, span = main_ref.shape
    lows = [lax.rem(lax.div(me, 2**bit), 2) for bit in range(len(send_refs))]
    for first in range(0, channels, rows):
        block = slice(first, first + rows)
        mixed = (
            key_value_ref[block].astype(F32) * block_scale(exp_ref[1, :, block] + exp_ref[2, :, block], span)
        ).astype(BF16)
        pulled = (query_cot_ref[block].astype(F32) * block_scale(exp_ref[0, :, block], span)).astype(BF16)
        for ref, later in [(main_ref, upper), (rest_ref, 1 - upper), *zip(send_refs, lows)]:
            ref[block] = jnp.where(later == 1, pulled, mixed)


def windows_kernel(
    n, rows, proj_ref, exp_ref, filt_ref, reach_ref, skip_ref, main_ref, rest_ref, high_ref, low_ref,
    recv_ref, deq_ref, base_ref, *rest
):
    win_refs, (taps, lens, gain) = rest[: n - 2], rest[n - 2 :]
    me = lax.axis_index("ctx")
    channels, seq_len = filt_ref.shape
    span = seq_len // n
    fscale = 1.0 / math.sqrt(seq_len)
    for group in range(3):
        deq_ref[group] = (proj_ref[group].astype(F32) * block_scale(exp_ref[group], span)).astype(BF16)
    upper = top_bit(n)
    lens[...] = reach_lens(reach_ref, seq_len)
    gain[...] = column(skip_ref) * (1.0 / fscale)

    @row_loop(channels, rows)
    def _(block):
        count = min(rows, channels)
        taps[0] = jnp.zeros((count, span), BF16)
        for b in range(n):
            lag = lax.broadcasted_iota(jnp.int32, (count, span), 1) + b * span
            taps[b + 1] = jnp.where(
                lag < lens[block], filt_ref[block, b * span : (b + 1) * span].astype(F32), 0.0
            ).astype(BF16)
        near = mm2(taps[1], high_ref[span:], low_ref[span:])
        near += gain[block] * high_ref[span : span + 1, :].astype(F32)
        wr, wi = near[:, :span], near[:, span:]
        for ref, later in ((main_ref, upper), (rest_ref, 1 - upper)):
            start = pl.multiple_of(later * span, span)
            spec = mm2(ref[block], high_ref[pl.ds(start, span), :], low_ref[pl.ds(start, span), :])
            xr, xi = spec[:, :span], spec[:, span:]
            turned = wi * (1 - 2 * later).astype(F32)
            base_ref[later, block, :span] = xr * wr - xi * turned
            base_ref[later, block, span:] = xr * turned + xi * wr
        for k in range(1, n):
            other = jnp.bitwise_xor(me, k)
            dist = jnp.abs(other - me)
            win = mm2(taps[dist], high_ref[:span], low_ref[:span]) + mm2(
                taps[dist + 1], high_ref[span:], low_ref[span:]
            )
            sign = jnp.where(other < me, 1.0, -1.0).astype(F32)
            wr, wi = win[:, :span], win[:, span:] * sign
            if k != early(n):
                slot = others(n).index(k)
                win_refs[slot][block, :span] = wr.astype(BF16)
                win_refs[slot][block, span:] = wi.astype(BF16)
                continue
            later = jnp.where(other > me, 1, 0)
            start = pl.multiple_of(later * span, span)
            spec = mm2(recv_ref[block], high_ref[pl.ds(start, span), :], low_ref[pl.ds(start, span), :])
            xr, xi = spec[:, :span], spec[:, span:]
            base_ref[later, block, :span] += xr * wr - xi * wi
            base_ref[later, block, span:] += xr * wi + xi * wr


def conv_kernel(n, seq_len, *refs):
    recv_refs, win_refs, refs = refs[: n - 2], refs[n - 2 : 2 * n - 4], refs[2 * n - 4 :]
    _, deq_ref, high_ref, inv_ref, acc, resp_ref, conv_ref, peak_ref = refs
    me = lax.axis_index("ctx")
    span = resp_ref.shape[1]
    fscale = 1.0 / math.sqrt(seq_len)
    for k, recv_ref, win_ref in zip(others(n), recv_refs, win_refs):
        later = jnp.where(jnp.bitwise_xor(me, k) > me, 1, 0)
        start = pl.multiple_of(later * span, span)
        spec = mm(recv_ref[...], high_ref[pl.ds(start, span), :])
        xr, xi = spec[:, :span], spec[:, span:]
        wr = win_ref[:, :span].astype(F32)
        wi = win_ref[:, span:].astype(F32)
        acc[later, :, :span] += xr * wr - xi * wi
        acc[later, :, span:] += xr * wi + xi * wr
    conv = mm(acc[0].astype(BF16), inv_ref[:, span:]) * fscale
    response = deq_ref[0].astype(F32) * conv
    resp_ref[...] = response
    conv_ref[...] = conv
    peak_ref[...] = jnp.max(jnp.abs(response), axis=0, keepdims=True)


def taps_kernel(n, seq_len, main_ref, rest_ref, reach_ref, high_ref, inv_ref, *refs):
    first_refs, second_refs, refs = refs[: n - 1], refs[n - 1 : 2 * n - 2], refs[2 * n - 2 :]
    peak_ref, out_refs, top_ref = refs[0], refs[1 : n + 1], refs[n + 1]
    mbuf, pbuf, mspec, pspec, acc, out = refs[n + 2 :]
    top_ref[...] = peak_ref[...]
    me = lax.axis_index("ctx")
    _, rows, span = mbuf.shape
    fscale = 1.0 / math.sqrt(seq_len)
    upper = top_bit(n)

    @pl.when(upper == 0)
    def _():
        mbuf[me] = main_ref[me]
        pbuf[me] = rest_ref[me]

    @pl.when(upper == 1)
    def _():
        mbuf[me] = rest_ref[me]
        pbuf[me] = main_ref[me]

    pbuf[n] = jnp.zeros((rows, span), BF16)
    for k in range(1, n):
        other = jnp.bitwise_xor(me, k)

        @pl.when(other < me)
        def _():
            mbuf[other] = first_refs[k - 1][me]
            pbuf[other] = second_refs[k - 1][...]

        @pl.when(other > me)
        def _():
            pbuf[other] = first_refs[k - 1][me]
            mbuf[other] = second_refs[k - 1][...]

    if rows % 16 == 0:
        flat = (n * rows, span)
        mspec[...] = mm(mbuf[...].reshape(flat), high_ref[:span]).reshape(mspec.shape)
        pair = jnp.concatenate([pbuf[:n].reshape(flat), pbuf[1:].reshape(flat)], axis=1)
        pspec[...] = mm(pair, high_ref[...]).reshape(pspec.shape)
    else:
        for b in range(n):
            mspec[b] = mm(mbuf[b], high_ref[:span])
            pspec[b] = mm(pbuf[b], high_ref[:span]) + mm(pbuf[b + 1], high_ref[span:])

    @row_loop(rows, rows)
    def _(tile):
        for lag_block in range(n):
            real = imag = 0.0
            for b in range(n - lag_block):
                ar, ai = mspec[b, tile, :span], mspec[b, tile, span:]
                br, bi = pspec[b + lag_block, tile, :span], pspec[b + lag_block, tile, span:]
                real += ar * br + ai * bi
                imag += ar * bi - ai * br
            acc[lag_block, tile, :span] = real.astype(BF16)
            acc[lag_block, tile, span:] = imag.astype(BF16)

    lens = reach_lens(reach_ref.at[me], seq_len)
    for lag_block in range(n):
        lag = lax.broadcasted_iota(jnp.int32, (rows, span), 1) + lag_block * span
        own = mm(acc[lag_block], inv_ref[:, :span]) * fscale
        out[lag_block] = jnp.where(lag < lens, own, 0.0).astype(BF16)
    for k in range(n):
        out_refs[k][...] = out[jnp.bitwise_xor(me, k)]


def pick_kernel(k, n, main_ref, rest_ref, *refs):
    me = lax.axis_index("ctx")
    other = jnp.bitwise_xor(me, k)
    out_ref = refs[-1]

    wanted = jnp.where(other > me, 1, 0)

    @pl.when(wanted == top_bit(n))
    def _():
        out_ref[...] = main_ref[other]

    @pl.when(wanted != top_bit(n))
    def _():
        out_ref[...] = rest_ref[other]


def grads_kernel(seq_len, deq_ref, cot_ref, conv_ref, acc_ref, inv_ref, grad_hbm, grad, grad_sem):
    span = cot_ref.shape[1]
    fscale = 1.0 / math.sqrt(seq_len)
    copies = []

    def send(slot, value):
        grad[slot] = value.astype(BF16)
        copies.append(pltpu.make_async_copy(grad.at[slot], grad_hbm.at[slot], grad_sem.at[slot]))
        copies[-1].start()

    send(0, cot_ref[...].astype(F32) * conv_ref[...])
    grad_mixed = mm(acc_ref[1].astype(BF16), inv_ref[:, :span]) * fscale
    send(1, grad_mixed * deq_ref[2].astype(F32))
    send(2, grad_mixed * deq_ref[1].astype(F32))
    for copy in copies:
        copy.wait()


def spread_kernel(n, *refs):
    part_refs, (near_ref, taps_hbm, peak_ref, taps, taps_sem) = refs[:n], refs[n:]
    me = lax.axis_index("ctx")
    peak_ref[...] = near_ref[...]
    copies = []
    for k in range(n):
        block = jnp.bitwise_xor(me, k)
        taps[block] = part_refs[k][...].astype(F32)
        copies.append(pltpu.make_async_copy(taps.at[block], taps_hbm.at[block], taps_sem.at[k]))
        copies[-1].start()
    for copy in copies:
        copy.wait()


def scale_kernel(resp_ref, near_ref, far_ref, out_ref, peak_ref):
    peak = jnp.maximum(near_ref[...], far_ref[...])
    peak_ref[...] = peak
    out_ref[...] = (resp_ref[...] * (1.0 / (peak + 1e-06))).astype(BF16)


def params(mib=32):
    return pltpu.CompilerParams(vmem_limit_bytes=int(mib * 2**20))


def body(proj, scale_exp, filt, reach, skip, cotangent):
    groups, channels, span = proj.shape
    n = lax.axis_size("ctx")
    ch_count = lax.axis_size("ch")
    seq_len = n * span
    blocks = scale_exp.shape[2]
    bits = max(1, (n - 1).bit_length())
    rows = channels
    parts = 2 if channels % 256 == 0 else 1
    share = channels // n
    shares = (n, share, span)
    high, low, inverse = (jnp.asarray(t) for t in fourier_tables(span))
    exps = jnp.transpose(scale_exp, (0, 2, 1))
    reach_row = reach.reshape(1, channels)
    skip_row = skip.reshape(1, channels)
    vmem = pl.BlockSpec(memory_space=pltpu.VMEM)
    hbm = pl.BlockSpec(memory_space=pltpu.HBM)
    remote = pl.BlockSpec(memory_space=pl.ANY)

    def shape(dims, dtype):
        return jax.ShapeDtypeStruct(dims, dtype)

    def call(kernel, name, ins, outs, mib=32, out_specs=None, **options):
        return pl.pallas_call(
            kernel,
            in_specs=ins,
            out_specs=out_specs or [vmem] * len(outs),
            out_shape=outs,
            compiler_params=params(mib),
            name=name,
            cost_estimate=COSTS.get(name),
            **options,
        )

    def swap(value, axis, k):
        return lax.ppermute(value, axis, [(j, j ^ k) for j in range(lax.axis_size(axis))])

    flat = shape((channels, span), BF16)
    part = shape((share, span), BF16)
    line = shape((1, span), F32)
    raw = call(
        functools.partial(load_kernel, parts),
        "load",
        [hbm] * 2,
        [flat] * 2,
        mib=LOAD_MIB,
        scratch_shapes=[
            pltpu.VMEM((3, channels, span), BF16),
            pltpu.VMEM((channels, span), BF16),
            pltpu.SemaphoreType.DMA((parts,)),
            pltpu.SemaphoreType.DMA((parts, 2)),
        ],
    )(proj, cotangent)
    main, rest, *sends = call(
        functools.partial(prep_kernel, n, rows), "prep", [vmem] * 3, [flat] * (1 + bits)
    )(*raw, exps)
    sends.append(main)
    first = [swap(sends[k.bit_length() - 1], "ctx", k) for k in range(1, n)]

    def pick(k, *after):
        return call(functools.partial(pick_kernel, k, n), "pick", [vmem] * 2 + [remote] * len(after), [part])(
            main.reshape(shares), rest.reshape(shares), *after
        )[0]

    second = {k: swap(pick(k), "ctx", k) for k in range(2, n)}

    wide = shape((channels, 2 * span), BF16)
    deq, base, *wins = call(
        functools.partial(windows_kernel, n, rows),
        "windows",
        [vmem] * 10,
        [shape((3, channels, span), BF16), shape((2, channels, 2 * span), F32)] + [wide] * (n - 2),
        scratch_shapes=[
            pltpu.VMEM((n + 1, rows, span), BF16),
            pltpu.VMEM((channels, 1), jnp.int32),
            pltpu.VMEM((channels, 1), F32),
        ],
    )(proj, exps, filt, reach_row, skip_row, main, rest, high, low, first[early(n) - 1])
    second[1] = swap(pick(1, first[early(n) - 1]), "ctx", 1)

    acc, response, conv, peak = call(
        functools.partial(conv_kernel, n, seq_len),
        "conv",
        [vmem] * (2 * n),
        [shape((2, channels, 2 * span), F32)] + [shape((channels, span), F32)] * 2 + [line],
        input_output_aliases={2 * n - 4: 0},
    )(*[first[k - 1] for k in others(n)], *wins, base, deq, high, inverse)

    far = swap(peak, "ch", 1)
    own_part, *parts_out, peak = call(
        functools.partial(taps_kernel, n, seq_len),
        "taps",
        [vmem] * (2 * n + 4),
        [part] * n + [line],
        scratch_shapes=[
            pltpu.VMEM(shares, BF16),
            pltpu.VMEM((n + 1, share, span), BF16),
            pltpu.VMEM((n, share, 2 * span), F32),
            pltpu.VMEM((n, share, 2 * span), F32),
            pltpu.VMEM((n, share, 2 * span), BF16),
            pltpu.VMEM(shares, BF16),
        ],
    )(
        main.reshape(shares), rest.reshape(shares), reach.reshape(n, 1, share), high, inverse,
        *[x.reshape(shares) for x in first], *[second[k] for k in range(1, n)], peak,
    )
    hop = 2
    while hop < ch_count:
        peak = jnp.maximum(peak, far)
        far = swap(peak, "ch", hop)
        hop *= 2
    parts_out = [swap(x, "ctx", k + 1) for k, x in enumerate(parts_out)]
    (gradients,) = call(
        functools.partial(grads_kernel, seq_len),
        "grads",
        [vmem] * 5,
        [shape((3, channels, span), BF16)],
        out_specs=[hbm],
        scratch_shapes=[pltpu.VMEM((3, channels, span), BF16), pltpu.SemaphoreType.DMA((3,))],
    )(deq, cotangent, conv, acc, inverse)
    filter_grad, peak = call(
        functools.partial(spread_kernel, n),
        "spread",
        [vmem] * (n + 1),
        [shape(shares, F32), line],
        out_specs=[hbm, vmem],
        scratch_shapes=[pltpu.VMEM(shares, F32), pltpu.SemaphoreType.DMA((n,))],
    )(own_part, *parts_out, peak)
    scaled_out, peak = call(scale_kernel, "scale", [vmem] * 3, [flat, line])(response, peak, far)
    return (scaled_out, peak.reshape(span), gradients, filter_grad.reshape(channels, span))


def solution(mesh):
    return jax.shard_map(
        body,
        mesh=mesh,
        in_specs=(
            P(None, "ch", "ctx"),
            P(None, "ch", "ctx"),
            P("ch", None),
            P("ch"),
            P("ch"),
            P("ch", "ctx"),
        ),
        out_specs=(P("ch", "ctx"), P("ctx"), P(None, "ch", "ctx"), P("ch", "ctx")),
        check_vma=False,
    )
```

```python
import functools
import math

import jax
import jax.numpy as jnp
import ml_dtypes
import numpy as np
from jax import lax
from jax.experimental import pallas as pl
from jax.experimental.pallas import tpu as pltpu
from jax.sharding import PartitionSpec as P

REACH_DIVISORS = (64, 32, 16, 4, 1)
LOAD_MIB = 53.5


def cost(flops):
    return pl.CostEstimate(flops=flops, bytes_accessed=10**6, transcendentals=0)


COSTS = {"load": cost(10**9), "grads": cost(10**9), "scale": cost(10**9)}
F32 = jnp.float32
BF16 = jnp.bfloat16


def fourier_tables(span):
    freq = np.arange(span)
    time = np.arange(2 * span)
    phase = ((2 * freq[None, :] + 1) * time[:, None]) % (4 * span)
    angle = phase * (math.pi / (2 * span))
    forward = np.concatenate([np.cos(angle), -np.sin(angle)], axis=1)
    high = forward.astype(ml_dtypes.bfloat16)
    low = (forward - high.astype(np.float64)).astype(ml_dtypes.bfloat16)
    inverse = (forward.T / span).astype(ml_dtypes.bfloat16)
    return high, low, inverse


def mm(left, right):
    return lax.dot_general(left, right, (((1,), (0,)), ((), ())), preferred_element_type=F32)


def mm2(left, high, low):
    return mm(left, high) + mm(left, low)


def block_scale(exps, span):
    blocks = exps.shape[0]
    block_len = span // blocks
    col = lax.broadcasted_iota(jnp.int32, (blocks, span), 1)
    row = lax.broadcasted_iota(jnp.int32, (blocks, span), 0)
    onehot = jnp.where(col // block_len == row, 1.0, 0.0).astype(BF16)
    scale = jnp.exp2(exps.astype(F32)).astype(BF16)
    return lax.dot_general(scale, onehot, (((0,), (0,)), ((), ())), preferred_element_type=F32)


def column(row_ref):
    row = row_ref[...]
    return jnp.transpose(jnp.broadcast_to(row, (8, row.shape[1])))[:, 0:1]


def reach_lens(reach_ref, seq_len):
    cls = column(reach_ref)
    out = jnp.zeros_like(cls)
    for index, div in enumerate(REACH_DIVISORS):
        out = jnp.where(cls == index, seq_len // div, out)
    return out


def cmul_parts(first, second, half):
    ar, ai = first[:, :half], first[:, half:]
    br, bi = second[:, :half], second[:, half:]
    return ar, ai, br, bi


def row_loop(total, step):
    def run(step_fn):
        if total <= step:
            step_fn(slice(0, total))
            return

        def one(i, carry):
            step_fn(pl.ds(pl.multiple_of(i * step, step), step))
            return carry

        lax.fori_loop(0, total // step, one, 0)

    return run


def early(n):
    return min(3, n - 1)


def others(n):
    return [k for k in range(1, n) if k != early(n)]


def top_bit(n):
    return lax.div(lax.axis_index("ctx"), (n + 1) // 2)


def load_kernel(n, proj_hbm, cot_hbm, raw_ref, left, right, sems):
    upper = top_bit(n)

    def pair(first, second):
        copies = [
            pltpu.make_async_copy(first, left, sems.at[0]),
            pltpu.make_async_copy(second, right, sems.at[1]),
        ]
        for copy in copies:
            copy.start()
        for copy in copies:
            copy.wait()

    @pl.when(upper == 0)
    def _():
        pair(proj_hbm.at[1], proj_hbm.at[2])

    @pl.when(upper == 1)
    def _():
        pair(proj_hbm.at[0], cot_hbm)

    raw_ref[...] = (left[...].astype(F32) * right[...].astype(F32)).astype(BF16)


def exponents(exp_ref, pulled):
    return jnp.where(pulled == 1, exp_ref[0], exp_ref[1] + exp_ref[2])


def main_kernel(n, raw_ref, exp_ref, main_ref):
    span = main_ref.shape[1]
    main_ref[...] = (raw_ref[...].astype(F32) * block_scale(exponents(exp_ref, top_bit(n)), span)).astype(BF16)


def rest_kernel(n, proj_ref, cot_ref, exp_ref, main_ref, rest_ref, *send_refs):
    me = lax.axis_index("ctx")
    upper = top_bit(n)
    span = main_ref.shape[1]
    scale = block_scale(exponents(exp_ref, 1 - upper), span)

    @pl.when(upper == 1)
    def _():
        rest_ref[...] = (proj_ref[1].astype(F32) * proj_ref[2].astype(F32) * scale).astype(BF16)

    @pl.when(upper == 0)
    def _():
        rest_ref[...] = (cot_ref[...].astype(F32) * proj_ref[0].astype(F32) * scale).astype(BF16)

    for bit, ref in enumerate(send_refs):
        low = lax.rem(lax.div(me, 2**bit), 2)

        @pl.when(low == upper)
        def _():
            ref[...] = main_ref[...]

        @pl.when(low != upper)
        def _():
            ref[...] = rest_ref[...]


def windows_kernel(
    n, rows, proj_ref, exp_ref, filt_ref, reach_ref, skip_ref, main_ref, rest_ref, high_ref, low_ref,
    recv_ref, deq_ref, base_ref, *rest
):
    win_refs, (taps, lens, gain) = rest[: n - 2], rest[n - 2 :]
    me = lax.axis_index("ctx")
    channels, seq_len = filt_ref.shape
    span = seq_len // n
    fscale = 1.0 / math.sqrt(seq_len)
    for group in range(3):
        deq_ref[group] = (proj_ref[group].astype(F32) * block_scale(exp_ref[group], span)).astype(BF16)
    upper = top_bit(n)
    lens[...] = reach_lens(reach_ref, seq_len)
    gain[...] = column(skip_ref) * (1.0 / fscale)

    @row_loop(channels, rows)
    def _(block):
        count = min(rows, channels)
        taps[0] = jnp.zeros((count, span), BF16)
        for b in range(n):
            lag = lax.broadcasted_iota(jnp.int32, (count, span), 1) + b * span
            taps[b + 1] = jnp.where(
                lag < lens[block], filt_ref[block, b * span : (b + 1) * span].astype(F32), 0.0
            ).astype(BF16)
        near = mm2(taps[1], high_ref[span:], low_ref[span:])
        near += gain[block] * high_ref[span : span + 1, :].astype(F32)
        wr, wi = near[:, :span], near[:, span:]
        for ref, later in ((main_ref, upper), (rest_ref, 1 - upper)):
            start = pl.multiple_of(later * span, span)
            spec = mm2(ref[block], high_ref[pl.ds(start, span), :], low_ref[pl.ds(start, span), :])
            xr, xi = spec[:, :span], spec[:, span:]
            turned = wi * (1 - 2 * later).astype(F32)
            base_ref[later, block, :span] = xr * wr - xi * turned
            base_ref[later, block, span:] = xr * turned + xi * wr
        for k in range(1, n):
            other = jnp.bitwise_xor(me, k)
            dist = jnp.abs(other - me)
            win = mm2(taps[dist], high_ref[:span], low_ref[:span]) + mm2(
                taps[dist + 1], high_ref[span:], low_ref[span:]
            )
            sign = jnp.where(other < me, 1.0, -1.0).astype(F32)
            wr, wi = win[:, :span], win[:, span:] * sign
            if k != early(n):
                slot = others(n).index(k)
                win_refs[slot][block, :span] = wr.astype(BF16)
                win_refs[slot][block, span:] = wi.astype(BF16)
                continue
            later = jnp.where(other > me, 1, 0)
            start = pl.multiple_of(later * span, span)
            spec = mm2(recv_ref[block], high_ref[pl.ds(start, span), :], low_ref[pl.ds(start, span), :])
            xr, xi = spec[:, :span], spec[:, span:]
            base_ref[later, block, :span] += xr * wr - xi * wi
            base_ref[later, block, span:] += xr * wi + xi * wr


def conv_kernel(n, seq_len, *refs):
    recv_refs, win_refs, refs = refs[: n - 2], refs[n - 2 : 2 * n - 4], refs[2 * n - 4 :]
    _, deq_ref, high_ref, inv_ref, acc, resp_ref, conv_ref, peak_ref = refs
    me = lax.axis_index("ctx")
    span = resp_ref.shape[1]
    fscale = 1.0 / math.sqrt(seq_len)
    for k, recv_ref, win_ref in zip(others(n), recv_refs, win_refs):
        later = jnp.where(jnp.bitwise_xor(me, k) > me, 1, 0)
        start = pl.multiple_of(later * span, span)
        spec = mm(recv_ref[...], high_ref[pl.ds(start, span), :])
        xr, xi = spec[:, :span], spec[:, span:]
        wr = win_ref[:, :span].astype(F32)
        wi = win_ref[:, span:].astype(F32)
        acc[later, :, :span] += xr * wr - xi * wi
        acc[later, :, span:] += xr * wi + xi * wr
    conv = mm(acc[0].astype(BF16), inv_ref[:, span:]) * fscale
    response = deq_ref[0].astype(F32) * conv
    resp_ref[...] = response
    conv_ref[...] = conv
    peak_ref[...] = jnp.max(jnp.abs(response), axis=0, keepdims=True)


def taps_kernel(n, seq_len, main_ref, rest_ref, reach_ref, high_ref, inv_ref, *refs):
    first_refs, second_refs, refs = refs[: n - 1], refs[n - 1 : 2 * n - 2], refs[2 * n - 2 :]
    peak_ref, out_refs, top_ref = refs[0], refs[1 : n + 1], refs[n + 1]
    mbuf, pbuf, mspec, pspec, acc, out = refs[n + 2 :]
    top_ref[...] = peak_ref[...]
    me = lax.axis_index("ctx")
    _, rows, span = mbuf.shape
    fscale = 1.0 / math.sqrt(seq_len)
    upper = top_bit(n)

    @pl.when(upper == 0)
    def _():
        mbuf[me] = main_ref[me]
        pbuf[me] = rest_ref[me]

    @pl.when(upper == 1)
    def _():
        mbuf[me] = rest_ref[me]
        pbuf[me] = main_ref[me]

    pbuf[n] = jnp.zeros((rows, span), BF16)
    for k in range(1, n):
        other = jnp.bitwise_xor(me, k)

        @pl.when(other < me)
        def _():
            mbuf[other] = first_refs[k - 1][me]
            pbuf[other] = second_refs[k - 1][...]

        @pl.when(other > me)
        def _():
            pbuf[other] = first_refs[k - 1][me]
            mbuf[other] = second_refs[k - 1][...]

    if rows % 16 == 0:
        flat = (n * rows, span)
        mspec[...] = mm(mbuf[...].reshape(flat), high_ref[:span]).reshape(mspec.shape)
        pair = jnp.concatenate([pbuf[:n].reshape(flat), pbuf[1:].reshape(flat)], axis=1)
        pspec[...] = mm(pair, high_ref[...]).reshape(pspec.shape)
    else:
        for b in range(n):
            mspec[b] = mm(mbuf[b], high_ref[:span])
            pspec[b] = mm(pbuf[b], high_ref[:span]) + mm(pbuf[b + 1], high_ref[span:])

    @row_loop(rows, rows)
    def _(tile):
        for lag_block in range(n):
            real = imag = 0.0
            for b in range(n - lag_block):
                ar, ai = mspec[b, tile, :span], mspec[b, tile, span:]
                br, bi = pspec[b + lag_block, tile, :span], pspec[b + lag_block, tile, span:]
                real += ar * br + ai * bi
                imag += ar * bi - ai * br
            acc[lag_block, tile, :span] = real.astype(BF16)
            acc[lag_block, tile, span:] = imag.astype(BF16)

    lens = reach_lens(reach_ref.at[me], seq_len)
    for lag_block in range(n):
        lag = lax.broadcasted_iota(jnp.int32, (rows, span), 1) + lag_block * span
        own = mm(acc[lag_block], inv_ref[:, :span]) * fscale
        out[lag_block] = jnp.where(lag < lens, own, 0.0).astype(BF16)
    for k in range(n):
        out_refs[k][...] = out[jnp.bitwise_xor(me, k)]


def pick_kernel(k, n, main_ref, rest_ref, *refs):
    me = lax.axis_index("ctx")
    other = jnp.bitwise_xor(me, k)
    out_ref = refs[-1]

    wanted = jnp.where(other > me, 1, 0)

    @pl.when(wanted == top_bit(n))
    def _():
        out_ref[...] = main_ref[other]

    @pl.when(wanted != top_bit(n))
    def _():
        out_ref[...] = rest_ref[other]


def grads_kernel(seq_len, deq_ref, cot_ref, conv_ref, acc_ref, inv_ref, grad_hbm, grad, grad_sem):
    span = cot_ref.shape[1]
    fscale = 1.0 / math.sqrt(seq_len)
    copies = []

    def send(slot, value):
        grad[slot] = value.astype(BF16)
        copies.append(pltpu.make_async_copy(grad.at[slot], grad_hbm.at[slot], grad_sem.at[slot]))
        copies[-1].start()

    send(0, cot_ref[...].astype(F32) * conv_ref[...])
    grad_mixed = mm(acc_ref[1].astype(BF16), inv_ref[:, :span]) * fscale
    send(1, grad_mixed * deq_ref[2].astype(F32))
    send(2, grad_mixed * deq_ref[1].astype(F32))
    for copy in copies:
        copy.wait()


def spread_kernel(ks, *refs):
    part_refs, (near_ref, taps_hbm, peak_ref, taps, taps_sem) = refs[: len(ks)], refs[len(ks) :]
    me = lax.axis_index("ctx")
    peak_ref[...] = near_ref[...]
    copies = []
    for slot, k in enumerate(ks):
        block = jnp.bitwise_xor(me, k)
        taps[block] = part_refs[slot][...].astype(F32)
        copies.append(pltpu.make_async_copy(taps.at[block], taps_hbm.at[block], taps_sem.at[slot]))
        copies[-1].start()
    for copy in copies:
        copy.wait()


def scale_kernel(resp_ref, near_ref, far_ref, out_ref, peak_ref):
    peak = jnp.maximum(near_ref[...], far_ref[...])
    peak_ref[...] = peak
    out_ref[...] = (resp_ref[...] * (1.0 / (peak + 1e-06))).astype(BF16)


def params(mib=32):
    return pltpu.CompilerParams(vmem_limit_bytes=int(mib * 2**20))


def body(proj, scale_exp, filt, reach, skip, cotangent):
    groups, channels, span = proj.shape
    n = lax.axis_size("ctx")
    ch_count = lax.axis_size("ch")
    seq_len = n * span
    blocks = scale_exp.shape[2]
    bits = max(1, (n - 1).bit_length())
    rows = channels
    share = channels // n
    shares = (n, share, span)
    high, low, inverse = (jnp.asarray(t) for t in fourier_tables(span))
    exps = jnp.transpose(scale_exp, (0, 2, 1))
    reach_row = reach.reshape(1, channels)
    skip_row = skip.reshape(1, channels)
    vmem = pl.BlockSpec(memory_space=pltpu.VMEM)
    hbm = pl.BlockSpec(memory_space=pltpu.HBM)
    remote = pl.BlockSpec(memory_space=pl.ANY)

    def shape(dims, dtype):
        return jax.ShapeDtypeStruct(dims, dtype)

    def call(kernel, name, ins, outs, mib=32, out_specs=None, **options):
        return pl.pallas_call(
            kernel,
            in_specs=ins,
            out_specs=out_specs or [vmem] * len(outs),
            out_shape=outs,
            compiler_params=params(mib),
            name=name,
            cost_estimate=COSTS.get(name),
            **options,
        )

    def swap(value, axis, k):
        return lax.ppermute(value, axis, [(j, j ^ k) for j in range(lax.axis_size(axis))])

    flat = shape((channels, span), BF16)
    part = shape((share, span), BF16)
    line = shape((1, span), F32)
    (raw,) = call(
        functools.partial(load_kernel, n),
        "load",
        [hbm] * 2,
        [flat],
        mib=LOAD_MIB,
        scratch_shapes=[
            pltpu.VMEM((channels, span), BF16),
            pltpu.VMEM((channels, span), BF16),
            pltpu.SemaphoreType.DMA((2,)),
        ],
    )(proj, cotangent)
    (main,) = call(functools.partial(main_kernel, n), "main", [vmem] * 2, [flat])(raw, exps)
    rest, *sends = call(functools.partial(rest_kernel, n), "rest", [vmem] * 4, [flat] * bits)(
        proj, cotangent, exps, main
    )
    sends.append(main)
    first = [swap(sends[k.bit_length() - 1], "ctx", k) for k in range(1, n)]

    def pick(k, *after):
        return call(functools.partial(pick_kernel, k, n), "pick", [vmem] * 2 + [remote] * len(after), [part])(
            main.reshape(shares), rest.reshape(shares), *after
        )[0]

    second = {k: swap(pick(k), "ctx", k) for k in range(2, n)}

    wide = shape((channels, 2 * span), BF16)
    deq, base, *wins = call(
        functools.partial(windows_kernel, n, rows),
        "windows",
        [vmem] * 10,
        [shape((3, channels, span), BF16), shape((2, channels, 2 * span), F32)] + [wide] * (n - 2),
        scratch_shapes=[
            pltpu.VMEM((n + 1, rows, span), BF16),
            pltpu.VMEM((channels, 1), jnp.int32),
            pltpu.VMEM((channels, 1), F32),
        ],
    )(proj, exps, filt, reach_row, skip_row, main, rest, high, low, first[early(n) - 1])
    second[1] = swap(pick(1, first[early(n) - 1]), "ctx", 1)

    acc, response, conv, peak = call(
        functools.partial(conv_kernel, n, seq_len),
        "conv",
        [vmem] * (2 * n),
        [shape((2, channels, 2 * span), F32)] + [shape((channels, span), F32)] * 2 + [line],
        input_output_aliases={2 * n - 4: 0},
    )(*[first[k - 1] for k in others(n)], *wins, base, deq, high, inverse)

    far = swap(peak, "ch", 1)
    own_part, *parts_out, peak = call(
        functools.partial(taps_kernel, n, seq_len),
        "taps",
        [vmem] * (2 * n + 4),
        [part] * n + [line],
        scratch_shapes=[
            pltpu.VMEM(shares, BF16),
            pltpu.VMEM((n + 1, share, span), BF16),
            pltpu.VMEM((n, share, 2 * span), F32),
            pltpu.VMEM((n, share, 2 * span), F32),
            pltpu.VMEM((n, share, 2 * span), BF16),
            pltpu.VMEM(shares, BF16),
        ],
    )(
        main.reshape(shares), rest.reshape(shares), reach.reshape(n, 1, share), high, inverse,
        *[x.reshape(shares) for x in first], *[second[k] for k in range(1, n)], peak,
    )
    hop = 2
    while hop < ch_count:
        peak = jnp.maximum(peak, far)
        far = swap(peak, "ch", hop)
        hop *= 2
    order = [*range(2, n), 1]
    parts_out = [swap(x, "ctx", k + 1) for k, x in enumerate(parts_out)]
    (gradients,) = call(
        functools.partial(grads_kernel, seq_len),
        "grads",
        [vmem] * 5,
        [shape((3, channels, span), BF16)],
        out_specs=[hbm],
        scratch_shapes=[pltpu.VMEM((3, channels, span), BF16), pltpu.SemaphoreType.DMA((3,))],
    )(deq, cotangent, conv, acc, inverse)
    filter_grad, peak = call(
        functools.partial(spread_kernel, (0, *order)),
        "spread",
        [vmem] * (n + 1),
        [shape(shares, F32), line],
        out_specs=[hbm, vmem],
        scratch_shapes=[pltpu.VMEM(shares, F32), pltpu.SemaphoreType.DMA((n,))],
    )(own_part, *[parts_out[k - 1] for k in order], peak)
    scaled_out, peak = call(scale_kernel, "scale", [vmem] * 3, [flat, line])(response, peak, far)
    return (scaled_out, peak.reshape(span), gradients, filter_grad.reshape(channels, span))


def solution(mesh):
    return jax.shard_map(
        body,
        mesh=mesh,
        in_specs=(
            P(None, "ch", "ctx"),
            P(None, "ch", "ctx"),
            P("ch", None),
            P("ch"),
            P("ch"),
            P("ch", "ctx"),
        ),
        out_specs=(P("ch", "ctx"), P("ctx"), P(None, "ch", "ctx"), P("ch", "ctx")),
        check_vma=False,
    )
```

```python
import functools
import math

import jax
import jax.numpy as jnp
import ml_dtypes
import numpy as np
from jax import lax
from jax.experimental import pallas as pl
from jax.experimental.pallas import tpu as pltpu
from jax.sharding import PartitionSpec as P

REACH_DIVISORS = (64, 32, 16, 4, 1)
LOAD_MIB = 53.5


def cost(flops):
    return pl.CostEstimate(flops=flops, bytes_accessed=10**6, transcendentals=0)


COSTS = {"load": cost(10**9), "grads": cost(10**9), "scale": cost(10**9)}
F32 = jnp.float32
BF16 = jnp.bfloat16


def fourier_tables(span):
    freq = np.arange(span)
    time = np.arange(2 * span)
    phase = ((2 * freq[None, :] + 1) * time[:, None]) % (4 * span)
    angle = phase * (math.pi / (2 * span))
    forward = np.concatenate([np.cos(angle), -np.sin(angle)], axis=1)
    high = forward.astype(ml_dtypes.bfloat16)
    low = (forward - high.astype(np.float64)).astype(ml_dtypes.bfloat16)
    inverse = (forward.T / span).astype(ml_dtypes.bfloat16)
    return high, low, inverse


def mm(left, right):
    return lax.dot_general(left, right, (((1,), (0,)), ((), ())), preferred_element_type=F32)


def mm2(left, high, low):
    return mm(left, high) + mm(left, low)


def block_scale(exps, span):
    blocks = exps.shape[0]
    block_len = span // blocks
    col = lax.broadcasted_iota(jnp.int32, (blocks, span), 1)
    row = lax.broadcasted_iota(jnp.int32, (blocks, span), 0)
    onehot = jnp.where(col // block_len == row, 1.0, 0.0).astype(BF16)
    scale = jnp.exp2(exps.astype(F32)).astype(BF16)
    return lax.dot_general(scale, onehot, (((0,), (0,)), ((), ())), preferred_element_type=F32)


def column(row_ref):
    row = row_ref[...]
    return jnp.transpose(jnp.broadcast_to(row, (8, row.shape[1])))[:, 0:1]


def reach_lens(reach_ref, seq_len):
    cls = column(reach_ref)
    out = jnp.zeros_like(cls)
    for index, div in enumerate(REACH_DIVISORS):
        out = jnp.where(cls == index, seq_len // div, out)
    return out


def cmul_parts(first, second, half):
    ar, ai = first[:, :half], first[:, half:]
    br, bi = second[:, :half], second[:, half:]
    return ar, ai, br, bi


def row_loop(total, step):
    def run(step_fn):
        if total <= step:
            step_fn(slice(0, total))
            return

        def one(i, carry):
            step_fn(pl.ds(pl.multiple_of(i * step, step), step))
            return carry

        lax.fori_loop(0, total // step, one, 0)

    return run


def early(n):
    return min(3, n - 1)


def others(n):
    return [k for k in range(1, n) if k != early(n)]


def top_bit(n):
    return lax.div(lax.axis_index("ctx"), (n + 1) // 2)


def load_kernel(n, proj_hbm, cot_hbm, raw_ref, left, right, sems):
    upper = top_bit(n)

    def pair(first, second):
        copies = [
            pltpu.make_async_copy(first, left, sems.at[0]),
            pltpu.make_async_copy(second, right, sems.at[1]),
        ]
        for copy in copies:
            copy.start()
        for copy in copies:
            copy.wait()

    @pl.when(upper == 0)
    def _():
        pair(proj_hbm.at[1], proj_hbm.at[2])

    @pl.when(upper == 1)
    def _():
        pair(proj_hbm.at[0], cot_hbm)

    raw_ref[...] = (left[...].astype(F32) * right[...].astype(F32)).astype(BF16)


def exponents(exp_ref, pulled):
    return jnp.where(pulled == 1, exp_ref[0], exp_ref[1] + exp_ref[2])


def main_kernel(n, raw_ref, exp_ref, main_ref):
    span = main_ref.shape[1]
    main_ref[...] = (raw_ref[...].astype(F32) * block_scale(exponents(exp_ref, top_bit(n)), span)).astype(BF16)


def rest_kernel(n, proj_ref, cot_ref, exp_ref, main_ref, rest_ref, *send_refs):
    me = lax.axis_index("ctx")
    upper = top_bit(n)
    span = main_ref.shape[1]
    scale = block_scale(exponents(exp_ref, 1 - upper), span)

    @pl.when(upper == 1)
    def _():
        rest_ref[...] = (proj_ref[1].astype(F32) * proj_ref[2].astype(F32) * scale).astype(BF16)

    @pl.when(upper == 0)
    def _():
        rest_ref[...] = (cot_ref[...].astype(F32) * proj_ref[0].astype(F32) * scale).astype(BF16)

    for bit, ref in enumerate(send_refs):
        low = lax.rem(lax.div(me, 2**bit), 2)

        @pl.when(low == upper)
        def _():
            ref[...] = main_ref[...]

        @pl.when(low != upper)
        def _():
            ref[...] = rest_ref[...]


def windows_kernel(
    n, rows, proj_ref, exp_ref, filt_ref, reach_ref, skip_ref, main_ref, rest_ref, high_ref, low_ref,
    recv_ref, deq_ref, base_ref, *rest
):
    win_refs, (taps, lens, gain) = rest[: n - 2], rest[n - 2 :]
    me = lax.axis_index("ctx")
    channels, seq_len = filt_ref.shape
    span = seq_len // n
    fscale = 1.0 / math.sqrt(seq_len)
    for group in range(3):
        deq_ref[group] = (proj_ref[group].astype(F32) * block_scale(exp_ref[group], span)).astype(BF16)
    upper = top_bit(n)
    lens[...] = reach_lens(reach_ref, seq_len)
    gain[...] = column(skip_ref) * (1.0 / fscale)

    @row_loop(channels, rows)
    def _(block):
        count = min(rows, channels)
        taps[0] = jnp.zeros((count, span), BF16)
        for b in range(n):
            lag = lax.broadcasted_iota(jnp.int32, (count, span), 1) + b * span
            taps[b + 1] = jnp.where(
                lag < lens[block], filt_ref[block, b * span : (b + 1) * span].astype(F32), 0.0
            ).astype(BF16)
        near = mm2(taps[1], high_ref[span:], low_ref[span:])
        near += gain[block] * high_ref[span : span + 1, :].astype(F32)
        wr, wi = near[:, :span], near[:, span:]
        for ref, later in ((main_ref, upper), (rest_ref, 1 - upper)):
            start = pl.multiple_of(later * span, span)
            spec = mm2(ref[block], high_ref[pl.ds(start, span), :], low_ref[pl.ds(start, span), :])
            xr, xi = spec[:, :span], spec[:, span:]
            turned = wi * (1 - 2 * later).astype(F32)
            base_ref[later, block, :span] = xr * wr - xi * turned
            base_ref[later, block, span:] = xr * turned + xi * wr
        for k in range(1, n):
            other = jnp.bitwise_xor(me, k)
            dist = jnp.abs(other - me)
            win = mm2(taps[dist], high_ref[:span], low_ref[:span]) + mm2(
                taps[dist + 1], high_ref[span:], low_ref[span:]
            )
            sign = jnp.where(other < me, 1.0, -1.0).astype(F32)
            wr, wi = win[:, :span], win[:, span:] * sign
            if k != early(n):
                slot = others(n).index(k)
                win_refs[slot][block, :span] = wr.astype(BF16)
                win_refs[slot][block, span:] = wi.astype(BF16)
                continue
            later = jnp.where(other > me, 1, 0)
            start = pl.multiple_of(later * span, span)
            spec = mm2(recv_ref[block], high_ref[pl.ds(start, span), :], low_ref[pl.ds(start, span), :])
            xr, xi = spec[:, :span], spec[:, span:]
            base_ref[later, block, :span] += xr * wr - xi * wi
            base_ref[later, block, span:] += xr * wi + xi * wr


def conv_kernel(n, seq_len, *refs):
    recv_refs, win_refs, refs = refs[: n - 2], refs[n - 2 : 2 * n - 4], refs[2 * n - 4 :]
    _, deq_ref, high_ref, inv_ref, acc, resp_ref, conv_ref, peak_ref = refs
    me = lax.axis_index("ctx")
    span = resp_ref.shape[1]
    fscale = 1.0 / math.sqrt(seq_len)
    for k, recv_ref, win_ref in zip(others(n), recv_refs, win_refs):
        later = jnp.where(jnp.bitwise_xor(me, k) > me, 1, 0)
        start = pl.multiple_of(later * span, span)
        spec = mm(recv_ref[...], high_ref[pl.ds(start, span), :])
        xr, xi = spec[:, :span], spec[:, span:]
        wr = win_ref[:, :span].astype(F32)
        wi = win_ref[:, span:].astype(F32)
        acc[later, :, :span] += xr * wr - xi * wi
        acc[later, :, span:] += xr * wi + xi * wr
    conv = mm(acc[0].astype(BF16), inv_ref[:, span:]) * fscale
    response = deq_ref[0].astype(F32) * conv
    resp_ref[...] = response
    conv_ref[...] = conv
    peak_ref[...] = jnp.max(jnp.abs(response), axis=0, keepdims=True)


def taps_kernel(n, seq_len, main_ref, rest_ref, reach_ref, high_ref, inv_ref, *refs):
    first_refs, second_refs, refs = refs[: n - 1], refs[n - 1 : 2 * n - 2], refs[2 * n - 2 :]
    peak_ref, out_refs, top_ref = refs[0], refs[1 : n + 1], refs[n + 1]
    mbuf, pbuf, mspec, pspec, acc, out = refs[n + 2 :]
    top_ref[...] = peak_ref[...]
    me = lax.axis_index("ctx")
    _, rows, span = mbuf.shape
    fscale = 1.0 / math.sqrt(seq_len)
    upper = top_bit(n)

    @pl.when(upper == 0)
    def _():
        mbuf[me] = main_ref[me]
        pbuf[me] = rest_ref[me]

    @pl.when(upper == 1)
    def _():
        mbuf[me] = rest_ref[me]
        pbuf[me] = main_ref[me]

    pbuf[n] = jnp.zeros((rows, span), BF16)
    for k in range(1, n):
        other = jnp.bitwise_xor(me, k)

        @pl.when(other < me)
        def _():
            mbuf[other] = first_refs[k - 1][me]
            pbuf[other] = second_refs[k - 1][...]

        @pl.when(other > me)
        def _():
            pbuf[other] = first_refs[k - 1][me]
            mbuf[other] = second_refs[k - 1][...]

    if rows % 16 == 0:
        flat = (n * rows, span)
        mspec[...] = mm(mbuf[...].reshape(flat), high_ref[:span]).reshape(mspec.shape)
        pair = jnp.concatenate([pbuf[:n].reshape(flat), pbuf[1:].reshape(flat)], axis=1)
        pspec[...] = mm(pair, high_ref[...]).reshape(pspec.shape)
    else:
        for b in range(n):
            mspec[b] = mm(mbuf[b], high_ref[:span])
            pspec[b] = mm(pbuf[b], high_ref[:span]) + mm(pbuf[b + 1], high_ref[span:])

    @row_loop(rows, rows)
    def _(tile):
        for lag_block in range(n):
            real = imag = 0.0
            for b in range(n - lag_block):
                ar, ai = mspec[b, tile, :span], mspec[b, tile, span:]
                br, bi = pspec[b + lag_block, tile, :span], pspec[b + lag_block, tile, span:]
                real += ar * br + ai * bi
                imag += ar * bi - ai * br
            acc[lag_block, tile, :span] = real.astype(BF16)
            acc[lag_block, tile, span:] = imag.astype(BF16)

    lens = reach_lens(reach_ref.at[me], seq_len)
    for lag_block in range(n):
        lag = lax.broadcasted_iota(jnp.int32, (rows, span), 1) + lag_block * span
        own = mm(acc[lag_block], inv_ref[:, :span]) * fscale
        out[lag_block] = jnp.where(lag < lens, own, 0.0).astype(BF16)
    for k in range(n):
        out_refs[k][...] = out[jnp.bitwise_xor(me, k)]


def pick_kernel(k, n, main_ref, rest_ref, *refs):
    me = lax.axis_index("ctx")
    other = jnp.bitwise_xor(me, k)
    out_ref = refs[-1]

    wanted = jnp.where(other > me, 1, 0)

    @pl.when(wanted == top_bit(n))
    def _():
        out_ref[...] = main_ref[other]

    @pl.when(wanted != top_bit(n))
    def _():
        out_ref[...] = rest_ref[other]


def back_kernel(seq_len, acc_ref, inv_ref, near_ref, out_ref, peak_ref):
    peak_ref[...] = near_ref[...]
    span = out_ref.shape[1]
    out_ref[...] = mm(acc_ref[1].astype(BF16), inv_ref[:, :span]) * (1.0 / math.sqrt(seq_len))


def grads_kernel(deq_ref, cot_ref, conv_ref, back_ref, grad_hbm, grad, grad_sem):
    copies = []

    def send(slot, value):
        grad[slot] = value.astype(BF16)
        copies.append(pltpu.make_async_copy(grad.at[slot], grad_hbm.at[slot], grad_sem.at[slot]))
        copies[-1].start()

    send(0, cot_ref[...].astype(F32) * conv_ref[...])
    grad_mixed = back_ref[...]
    send(1, grad_mixed * deq_ref[2].astype(F32))
    send(2, grad_mixed * deq_ref[1].astype(F32))
    for copy in copies:
        copy.wait()


def spread_kernel(ks, *refs):
    part_refs, (near_ref, taps_hbm, peak_ref, taps, taps_sem) = refs[: len(ks)], refs[len(ks) :]
    me = lax.axis_index("ctx")
    peak_ref[...] = near_ref[...]
    copies = []
    for slot, k in enumerate(ks):
        block = jnp.bitwise_xor(me, k)
        taps[block] = part_refs[slot][...].astype(F32)
        copies.append(pltpu.make_async_copy(taps.at[block], taps_hbm.at[block], taps_sem.at[slot]))
        copies[-1].start()
    for copy in copies:
        copy.wait()


def scale_kernel(resp_ref, near_ref, far_ref, out_ref, peak_ref):
    peak = jnp.maximum(near_ref[...], far_ref[...])
    peak_ref[...] = peak
    out_ref[...] = (resp_ref[...] * (1.0 / (peak + 1e-06))).astype(BF16)


def params(mib=32):
    return pltpu.CompilerParams(vmem_limit_bytes=int(mib * 2**20))


def body(proj, scale_exp, filt, reach, skip, cotangent):
    groups, channels, span = proj.shape
    n = lax.axis_size("ctx")
    ch_count = lax.axis_size("ch")
    seq_len = n * span
    blocks = scale_exp.shape[2]
    bits = max(1, (n - 1).bit_length())
    rows = channels
    share = channels // n
    shares = (n, share, span)
    high, low, inverse = (jnp.asarray(t) for t in fourier_tables(span))
    exps = jnp.transpose(scale_exp, (0, 2, 1))
    reach_row = reach.reshape(1, channels)
    skip_row = skip.reshape(1, channels)
    vmem = pl.BlockSpec(memory_space=pltpu.VMEM)
    hbm = pl.BlockSpec(memory_space=pltpu.HBM)
    remote = pl.BlockSpec(memory_space=pl.ANY)

    def shape(dims, dtype):
        return jax.ShapeDtypeStruct(dims, dtype)

    def call(kernel, name, ins, outs, mib=32, out_specs=None, **options):
        return pl.pallas_call(
            kernel,
            in_specs=ins,
            out_specs=out_specs or [vmem] * len(outs),
            out_shape=outs,
            compiler_params=params(mib),
            name=name,
            cost_estimate=COSTS.get(name),
            **options,
        )

    def swap(value, axis, k):
        return lax.ppermute(value, axis, [(j, j ^ k) for j in range(lax.axis_size(axis))])

    flat = shape((channels, span), BF16)
    part = shape((share, span), BF16)
    line = shape((1, span), F32)
    (raw,) = call(
        functools.partial(load_kernel, n),
        "load",
        [hbm] * 2,
        [flat],
        mib=LOAD_MIB,
        scratch_shapes=[
            pltpu.VMEM((channels, span), BF16),
            pltpu.VMEM((channels, span), BF16),
            pltpu.SemaphoreType.DMA((2,)),
        ],
    )(proj, cotangent)
    (main,) = call(functools.partial(main_kernel, n), "main", [vmem] * 2, [flat])(raw, exps)
    rest, *sends = call(functools.partial(rest_kernel, n), "rest", [vmem] * 4, [flat] * bits)(
        proj, cotangent, exps, main
    )
    sends.append(main)
    first = [swap(sends[k.bit_length() - 1], "ctx", k) for k in range(1, n)]

    def pick(k, *after):
        return call(functools.partial(pick_kernel, k, n), "pick", [vmem] * 2 + [remote] * len(after), [part])(
            main.reshape(shares), rest.reshape(shares), *after
        )[0]

    second = {k: swap(pick(k), "ctx", k) for k in range(2, n)}

    wide = shape((channels, 2 * span), BF16)
    deq, base, *wins = call(
        functools.partial(windows_kernel, n, rows),
        "windows",
        [vmem] * 10,
        [shape((3, channels, span), BF16), shape((2, channels, 2 * span), F32)] + [wide] * (n - 2),
        scratch_shapes=[
            pltpu.VMEM((n + 1, rows, span), BF16),
            pltpu.VMEM((channels, 1), jnp.int32),
            pltpu.VMEM((channels, 1), F32),
        ],
    )(proj, exps, filt, reach_row, skip_row, main, rest, high, low, first[early(n) - 1])
    second[1] = swap(pick(1, first[early(n) - 1]), "ctx", 1)

    acc, response, conv, peak = call(
        functools.partial(conv_kernel, n, seq_len),
        "conv",
        [vmem] * (2 * n),
        [shape((2, channels, 2 * span), F32)] + [shape((channels, span), F32)] * 2 + [line],
        input_output_aliases={2 * n - 4: 0},
    )(*[first[k - 1] for k in others(n)], *wins, base, deq, high, inverse)

    far = swap(peak, "ch", 1)
    back, peak = call(
        functools.partial(back_kernel, seq_len),
        "back",
        [vmem] * 3,
        [shape((channels, span), F32), line],
    )(acc, inverse, peak)
    own_part, *parts_out, peak = call(
        functools.partial(taps_kernel, n, seq_len),
        "taps",
        [vmem] * (2 * n + 4),
        [part] * n + [line],
        scratch_shapes=[
            pltpu.VMEM(shares, BF16),
            pltpu.VMEM((n + 1, share, span), BF16),
            pltpu.VMEM((n, share, 2 * span), F32),
            pltpu.VMEM((n, share, 2 * span), F32),
            pltpu.VMEM((n, share, 2 * span), BF16),
            pltpu.VMEM(shares, BF16),
        ],
    )(
        main.reshape(shares), rest.reshape(shares), reach.reshape(n, 1, share), high, inverse,
        *[x.reshape(shares) for x in first], *[second[k] for k in range(1, n)], peak,
    )
    hop = 2
    while hop < ch_count:
        peak = jnp.maximum(peak, far)
        far = swap(peak, "ch", hop)
        hop *= 2
    order = [*range(2, n), 1]
    parts_out = [swap(x, "ctx", k + 1) for k, x in enumerate(parts_out)]
    (gradients,) = call(
        grads_kernel,
        "grads",
        [vmem] * 4,
        [shape((3, channels, span), BF16)],
        out_specs=[hbm],
        scratch_shapes=[pltpu.VMEM((3, channels, span), BF16), pltpu.SemaphoreType.DMA((3,))],
    )(deq, cotangent, conv, back)
    filter_grad, peak = call(
        functools.partial(spread_kernel, (0, *order)),
        "spread",
        [vmem] * (n + 1),
        [shape(shares, F32), line],
        out_specs=[hbm, vmem],
        scratch_shapes=[pltpu.VMEM(shares, F32), pltpu.SemaphoreType.DMA((n,))],
    )(own_part, *[parts_out[k - 1] for k in order], peak)
    scaled_out, peak = call(scale_kernel, "scale", [vmem] * 3, [flat, line])(response, peak, far)
    return (scaled_out, peak.reshape(span), gradients, filter_grad.reshape(channels, span))


def solution(mesh):
    return jax.shard_map(
        body,
        mesh=mesh,
        in_specs=(
            P(None, "ch", "ctx"),
            P(None, "ch", "ctx"),
            P("ch", None),
            P("ch"),
            P("ch"),
            P("ch", "ctx"),
        ),
        out_specs=(P("ch", "ctx"), P("ctx"), P(None, "ch", "ctx"), P("ch", "ctx")),
        check_vma=False,
    )
```

```python
import functools
import math

import jax
import jax.numpy as jnp
import ml_dtypes
import numpy as np
from jax import lax
from jax.experimental import pallas as pl
from jax.experimental.pallas import tpu as pltpu
from jax.sharding import PartitionSpec as P

REACH_DIVISORS = (64, 32, 16, 4, 1)
LOAD_MIB = 53.5


def cost(flops):
    return pl.CostEstimate(flops=flops, bytes_accessed=10**6, transcendentals=0)


COSTS = {"load": cost(10**9), "grads": cost(10**9), "scale": cost(10**9)}
F32 = jnp.float32
BF16 = jnp.bfloat16


def fourier_tables(span):
    freq = np.arange(span)
    time = np.arange(2 * span)
    phase = ((2 * freq[None, :] + 1) * time[:, None]) % (4 * span)
    angle = phase * (math.pi / (2 * span))
    forward = np.concatenate([np.cos(angle), -np.sin(angle)], axis=1)
    high = forward.astype(ml_dtypes.bfloat16)
    low = (forward - high.astype(np.float64)).astype(ml_dtypes.bfloat16)
    inverse = (forward.T / span).astype(ml_dtypes.bfloat16)
    return high, low, inverse


def mm(left, right):
    return lax.dot_general(left, right, (((1,), (0,)), ((), ())), preferred_element_type=F32)


def mm2(left, high, low):
    return mm(left, high) + mm(left, low)


def block_scale(exps, span):
    blocks = exps.shape[0]
    block_len = span // blocks
    col = lax.broadcasted_iota(jnp.int32, (blocks, span), 1)
    row = lax.broadcasted_iota(jnp.int32, (blocks, span), 0)
    onehot = jnp.where(col // block_len == row, 1.0, 0.0).astype(BF16)
    scale = jnp.exp2(exps.astype(F32)).astype(BF16)
    return lax.dot_general(scale, onehot, (((0,), (0,)), ((), ())), preferred_element_type=F32)


def column(row_ref):
    row = row_ref[...]
    return jnp.transpose(jnp.broadcast_to(row, (8, row.shape[1])))[:, 0:1]


def reach_lens(reach_ref, seq_len):
    cls = column(reach_ref)
    out = jnp.zeros_like(cls)
    for index, div in enumerate(REACH_DIVISORS):
        out = jnp.where(cls == index, seq_len // div, out)
    return out


def cmul_parts(first, second, half):
    ar, ai = first[:, :half], first[:, half:]
    br, bi = second[:, :half], second[:, half:]
    return ar, ai, br, bi


def row_loop(total, step):
    def run(step_fn):
        if total <= step:
            step_fn(slice(0, total))
            return

        def one(i, carry):
            step_fn(pl.ds(pl.multiple_of(i * step, step), step))
            return carry

        lax.fori_loop(0, total // step, one, 0)

    return run


def early(n):
    return min(3, n - 1)


def others(n):
    return [k for k in range(1, n) if k != early(n)]


def top_bit(n):
    return lax.div(lax.axis_index("ctx"), (n + 1) // 2)


def load_kernel(n, proj_hbm, cot_hbm, raw_ref, left, right, sems):
    upper = top_bit(n)

    def pair(first, second):
        copies = [
            pltpu.make_async_copy(first, left, sems.at[0]),
            pltpu.make_async_copy(second, right, sems.at[1]),
        ]
        for copy in copies:
            copy.start()
        for copy in copies:
            copy.wait()

    @pl.when(upper == 0)
    def _():
        pair(proj_hbm.at[1], proj_hbm.at[2])

    @pl.when(upper == 1)
    def _():
        pair(proj_hbm.at[0], cot_hbm)

    raw_ref[...] = (left[...].astype(F32) * right[...].astype(F32)).astype(BF16)


def exponents(exp_ref, pulled):
    return jnp.where(pulled == 1, exp_ref[0], exp_ref[1] + exp_ref[2])


def main_kernel(n, raw_ref, exp_ref, main_ref):
    span = main_ref.shape[1]
    main_ref[...] = (raw_ref[...].astype(F32) * block_scale(exponents(exp_ref, top_bit(n)), span)).astype(BF16)


def rest_kernel(n, proj_ref, cot_ref, exp_ref, main_ref, rest_ref, *send_refs):
    me = lax.axis_index("ctx")
    upper = top_bit(n)
    span = main_ref.shape[1]
    scale = block_scale(exponents(exp_ref, 1 - upper), span)

    @pl.when(upper == 1)
    def _():
        rest_ref[...] = (proj_ref[1].astype(F32) * proj_ref[2].astype(F32) * scale).astype(BF16)

    @pl.when(upper == 0)
    def _():
        rest_ref[...] = (cot_ref[...].astype(F32) * proj_ref[0].astype(F32) * scale).astype(BF16)

    for bit, ref in enumerate(send_refs):
        low = lax.rem(lax.div(me, 2**bit), 2)

        @pl.when(low == upper)
        def _():
            ref[...] = main_ref[...]

        @pl.when(low != upper)
        def _():
            ref[...] = rest_ref[...]


def windows_kernel(
    n, rows, proj_ref, exp_ref, filt_ref, reach_ref, skip_ref, main_ref, rest_ref, high_ref, low_ref,
    recv_ref, deq_ref, base_ref, *rest
):
    win_refs, (taps, lens, gain) = rest[: n - 2], rest[n - 2 :]
    me = lax.axis_index("ctx")
    channels, seq_len = filt_ref.shape
    span = seq_len // n
    fscale = 1.0 / math.sqrt(seq_len)
    for group in range(3):
        deq_ref[group] = (proj_ref[group].astype(F32) * block_scale(exp_ref[group], span)).astype(BF16)
    upper = top_bit(n)
    lens[...] = reach_lens(reach_ref, seq_len)
    gain[...] = column(skip_ref) * (1.0 / fscale)

    @row_loop(channels, rows)
    def _(block):
        count = min(rows, channels)
        taps[0] = jnp.zeros((count, span), BF16)
        for b in range(n):
            lag = lax.broadcasted_iota(jnp.int32, (count, span), 1) + b * span
            taps[b + 1] = jnp.where(
                lag < lens[block], filt_ref[block, b * span : (b + 1) * span].astype(F32), 0.0
            ).astype(BF16)
        near = mm2(taps[1], high_ref[span:], low_ref[span:])
        near += gain[block] * high_ref[span : span + 1, :].astype(F32)
        wr, wi = near[:, :span], near[:, span:]
        for ref, later in ((main_ref, upper), (rest_ref, 1 - upper)):
            start = pl.multiple_of(later * span, span)
            spec = mm2(ref[block], high_ref[pl.ds(start, span), :], low_ref[pl.ds(start, span), :])
            xr, xi = spec[:, :span], spec[:, span:]
            turned = wi * (1 - 2 * later).astype(F32)
            base_ref[later, block, :span] = xr * wr - xi * turned
            base_ref[later, block, span:] = xr * turned + xi * wr
        for k in range(1, n):
            other = jnp.bitwise_xor(me, k)
            dist = jnp.abs(other - me)
            win = mm2(taps[dist], high_ref[:span], low_ref[:span]) + mm2(
                taps[dist + 1], high_ref[span:], low_ref[span:]
            )
            sign = jnp.where(other < me, 1.0, -1.0).astype(F32)
            wr, wi = win[:, :span], win[:, span:] * sign
            if k != early(n):
                slot = others(n).index(k)
                win_refs[slot][block, :span] = wr.astype(BF16)
                win_refs[slot][block, span:] = wi.astype(BF16)
                continue
            later = jnp.where(other > me, 1, 0)
            start = pl.multiple_of(later * span, span)
            spec = mm2(recv_ref[block], high_ref[pl.ds(start, span), :], low_ref[pl.ds(start, span), :])
            xr, xi = spec[:, :span], spec[:, span:]
            base_ref[later, block, :span] += xr * wr - xi * wi
            base_ref[later, block, span:] += xr * wi + xi * wr


def conv_kernel(n, seq_len, *refs):
    recv_refs, win_refs, refs = refs[: n - 2], refs[n - 2 : 2 * n - 4], refs[2 * n - 4 :]
    _, deq_ref, high_ref, inv_ref, acc, resp_ref, conv_ref, peak_ref = refs
    me = lax.axis_index("ctx")
    span = resp_ref.shape[1]
    fscale = 1.0 / math.sqrt(seq_len)
    for k, recv_ref, win_ref in zip(others(n), recv_refs, win_refs):
        later = jnp.where(jnp.bitwise_xor(me, k) > me, 1, 0)
        start = pl.multiple_of(later * span, span)
        spec = mm(recv_ref[...], high_ref[pl.ds(start, span), :])
        xr, xi = spec[:, :span], spec[:, span:]
        wr = win_ref[:, :span].astype(F32)
        wi = win_ref[:, span:].astype(F32)
        acc[later, :, :span] += xr * wr - xi * wi
        acc[later, :, span:] += xr * wi + xi * wr
    conv = mm(acc[0].astype(BF16), inv_ref[:, span:]) * fscale
    response = deq_ref[0].astype(F32) * conv
    resp_ref[...] = response
    conv_ref[...] = conv
    peak_ref[...] = jnp.max(jnp.abs(response), axis=0, keepdims=True)


def taps_kernel(n, seq_len, main_ref, rest_ref, reach_ref, high_ref, inv_ref, *refs):
    first_refs, second_refs, refs = refs[: n - 1], refs[n - 1 : 2 * n - 2], refs[2 * n - 2 :]
    peak_ref, out_refs, top_ref = refs[0], refs[1 : n + 1], refs[n + 1]
    mbuf, pbuf, mspec, pspec, acc, out = refs[n + 2 :]
    top_ref[...] = peak_ref[...]
    me = lax.axis_index("ctx")
    _, rows, span = mbuf.shape
    fscale = 1.0 / math.sqrt(seq_len)
    upper = top_bit(n)

    @pl.when(upper == 0)
    def _():
        mbuf[me] = main_ref[me]
        pbuf[me] = rest_ref[me]

    @pl.when(upper == 1)
    def _():
        mbuf[me] = rest_ref[me]
        pbuf[me] = main_ref[me]

    pbuf[n] = jnp.zeros((rows, span), BF16)
    for k in range(1, n):
        other = jnp.bitwise_xor(me, k)

        @pl.when(other < me)
        def _():
            mbuf[other] = first_refs[k - 1][me]
            pbuf[other] = second_refs[k - 1][...]

        @pl.when(other > me)
        def _():
            pbuf[other] = first_refs[k - 1][me]
            mbuf[other] = second_refs[k - 1][...]

    if rows % 16 == 0:
        flat = (n * rows, span)
        mspec[...] = mm(mbuf[...].reshape(flat), high_ref[:span]).reshape(mspec.shape)
        pair = jnp.concatenate([pbuf[:n].reshape(flat), pbuf[1:].reshape(flat)], axis=1)
        pspec[...] = mm(pair, high_ref[...]).reshape(pspec.shape)
    else:
        for b in range(n):
            mspec[b] = mm(mbuf[b], high_ref[:span])
            pspec[b] = mm(pbuf[b], high_ref[:span]) + mm(pbuf[b + 1], high_ref[span:])

    @row_loop(rows, rows)
    def _(tile):
        for lag_block in range(n):
            real = imag = 0.0
            for b in range(n - lag_block):
                ar, ai = mspec[b, tile, :span], mspec[b, tile, span:]
                br, bi = pspec[b + lag_block, tile, :span], pspec[b + lag_block, tile, span:]
                real += ar * br + ai * bi
                imag += ar * bi - ai * br
            acc[lag_block, tile, :span] = real.astype(BF16)
            acc[lag_block, tile, span:] = imag.astype(BF16)

    lens = reach_lens(reach_ref.at[me], seq_len)
    for lag_block in range(n):
        lag = lax.broadcasted_iota(jnp.int32, (rows, span), 1) + lag_block * span
        own = mm(acc[lag_block], inv_ref[:, :span]) * fscale
        out[lag_block] = jnp.where(lag < lens, own, 0.0).astype(BF16)
    for k in range(n):
        out_refs[k][...] = out[jnp.bitwise_xor(me, k)]


def pick_kernel(k, n, main_ref, rest_ref, *refs):
    me = lax.axis_index("ctx")
    other = jnp.bitwise_xor(me, k)
    out_ref = refs[-1]

    wanted = jnp.where(other > me, 1, 0)

    @pl.when(wanted == top_bit(n))
    def _():
        out_ref[...] = main_ref[other]

    @pl.when(wanted != top_bit(n))
    def _():
        out_ref[...] = rest_ref[other]


def back_kernel(seq_len, acc_ref, inv_ref, near_ref, out_ref, peak_ref):
    peak_ref[...] = near_ref[...]
    span = out_ref.shape[1]
    out_ref[...] = mm(acc_ref[1].astype(BF16), inv_ref[:, :span]) * (1.0 / math.sqrt(seq_len))


def grads_kernel(deq_ref, cot_ref, conv_ref, back_ref, grad_hbm, grad, grad_sem):
    copies = []

    def send(slot, value):
        grad[slot] = value.astype(BF16)
        copies.append(pltpu.make_async_copy(grad.at[slot], grad_hbm.at[slot], grad_sem.at[slot]))
        copies[-1].start()

    send(0, cot_ref[...].astype(F32) * conv_ref[...])
    grad_mixed = back_ref[...]
    send(1, grad_mixed * deq_ref[2].astype(F32))
    send(2, grad_mixed * deq_ref[1].astype(F32))
    for copy in copies:
        copy.wait()


def spread_kernel(ks, *refs):
    part_refs, (near_ref, taps_hbm, peak_ref, taps, taps_sem) = refs[: len(ks)], refs[len(ks) :]
    me = lax.axis_index("ctx")
    peak_ref[...] = near_ref[...]
    copies = []
    for slot, k in enumerate(ks):
        block = jnp.bitwise_xor(me, k)
        taps[block] = part_refs[slot][...].astype(F32)
        copies.append(pltpu.make_async_copy(taps.at[block], taps_hbm.at[block], taps_sem.at[slot]))
        copies[-1].start()
    for copy in copies:
        copy.wait()


def scale_kernel(resp_ref, near_ref, far_ref, out_ref, peak_ref):
    peak = jnp.maximum(near_ref[...], far_ref[...])
    peak_ref[...] = peak
    out_ref[...] = (resp_ref[...] * (1.0 / (peak + 1e-06))).astype(BF16)


def params(mib=32):
    return pltpu.CompilerParams(vmem_limit_bytes=int(mib * 2**20))


def body(proj, scale_exp, filt, reach, skip, cotangent):
    groups, channels, span = proj.shape
    n = lax.axis_size("ctx")
    ch_count = lax.axis_size("ch")
    seq_len = n * span
    blocks = scale_exp.shape[2]
    bits = max(1, (n - 1).bit_length())
    rows = channels
    share = channels // n
    shares = (n, share, span)
    high, low, inverse = (jnp.asarray(t) for t in fourier_tables(span))
    exps = jnp.transpose(scale_exp, (0, 2, 1))
    reach_row = reach.reshape(1, channels)
    skip_row = skip.reshape(1, channels)
    vmem = pl.BlockSpec(memory_space=pltpu.VMEM)
    hbm = pl.BlockSpec(memory_space=pltpu.HBM)
    remote = pl.BlockSpec(memory_space=pl.ANY)

    def shape(dims, dtype):
        return jax.ShapeDtypeStruct(dims, dtype)

    def call(kernel, name, ins, outs, mib=32, out_specs=None, **options):
        return pl.pallas_call(
            kernel,
            in_specs=ins,
            out_specs=out_specs or [vmem] * len(outs),
            out_shape=outs,
            compiler_params=params(mib),
            name=name,
            cost_estimate=COSTS.get(name),
            **options,
        )

    def swap(value, axis, k):
        return lax.ppermute(value, axis, [(j, j ^ k) for j in range(lax.axis_size(axis))])

    flat = shape((channels, span), BF16)
    part = shape((share, span), BF16)
    line = shape((1, span), F32)
    (raw,) = call(
        functools.partial(load_kernel, n),
        "load",
        [hbm] * 2,
        [flat],
        mib=LOAD_MIB,
        scratch_shapes=[
            pltpu.VMEM((channels, span), BF16),
            pltpu.VMEM((channels, span), BF16),
            pltpu.SemaphoreType.DMA((2,)),
        ],
    )(proj, cotangent)
    (main,) = call(functools.partial(main_kernel, n), "main", [vmem] * 2, [flat])(raw, exps)
    rest, *sends = call(functools.partial(rest_kernel, n), "rest", [vmem] * 4, [flat] * bits)(
        proj, cotangent, exps, main
    )
    sends.append(main)
    first = [swap(sends[k.bit_length() - 1], "ctx", k) for k in range(1, n)]

    def pick(k, *after):
        return call(functools.partial(pick_kernel, k, n), "pick", [vmem] * 2 + [remote] * len(after), [part])(
            main.reshape(shares), rest.reshape(shares), *after
        )[0]

    second = {k: swap(pick(k), "ctx", k) for k in range(2, n)}

    wide = shape((channels, 2 * span), BF16)
    deq, base, *wins = call(
        functools.partial(windows_kernel, n, rows),
        "windows",
        [vmem] * 10,
        [shape((3, channels, span), BF16), shape((2, channels, 2 * span), F32)] + [wide] * (n - 2),
        scratch_shapes=[
            pltpu.VMEM((n + 1, rows, span), BF16),
            pltpu.VMEM((channels, 1), jnp.int32),
            pltpu.VMEM((channels, 1), F32),
        ],
    )(proj, exps, filt, reach_row, skip_row, main, rest, high, low, first[early(n) - 1])
    second[1] = swap(pick(1, first[early(n) - 1]), "ctx", 1)

    acc, response, conv, peak = call(
        functools.partial(conv_kernel, n, seq_len),
        "conv",
        [vmem] * (2 * n),
        [shape((2, channels, 2 * span), F32)] + [shape((channels, span), F32)] * 2 + [line],
        input_output_aliases={2 * n - 4: 0},
    )(*[first[k - 1] for k in others(n)], *wins, base, deq, high, inverse)

    far = swap(peak, "ch", 1)
    back, peak = call(
        functools.partial(back_kernel, seq_len),
        "back",
        [vmem] * 3,
        [shape((channels, span), F32), line],
    )(acc, inverse, peak)
    own_part, *parts_out, peak = call(
        functools.partial(taps_kernel, n, seq_len),
        "taps",
        [vmem] * (2 * n + 4),
        [part] * n + [line],
        scratch_shapes=[
            pltpu.VMEM(shares, BF16),
            pltpu.VMEM((n + 1, share, span), BF16),
            pltpu.VMEM((n, share, 2 * span), F32),
            pltpu.VMEM((n, share, 2 * span), F32),
            pltpu.VMEM((n, share, 2 * span), BF16),
            pltpu.VMEM(shares, BF16),
        ],
    )(
        main.reshape(shares), rest.reshape(shares), reach.reshape(n, 1, share), high, inverse,
        *[x.reshape(shares) for x in first], *[second[k] for k in range(1, n)], peak,
    )
    hop = 2
    while hop < ch_count:
        peak = jnp.maximum(peak, far)
        far = swap(peak, "ch", hop)
        hop *= 2
    order = [*range(n - 1, 0, -1)]
    parts_out = [swap(x, "ctx", k + 1) for k, x in enumerate(parts_out)]
    (gradients,) = call(
        grads_kernel,
        "grads",
        [vmem] * 4,
        [shape((3, channels, span), BF16)],
        out_specs=[hbm],
        scratch_shapes=[pltpu.VMEM((3, channels, span), BF16), pltpu.SemaphoreType.DMA((3,))],
    )(deq, cotangent, conv, back)
    filter_grad, peak = call(
        functools.partial(spread_kernel, (0, *order)),
        "spread",
        [vmem] * (n + 1),
        [shape(shares, F32), line],
        out_specs=[hbm, vmem],
        scratch_shapes=[pltpu.VMEM(shares, F32), pltpu.SemaphoreType.DMA((n,))],
    )(own_part, *[parts_out[k - 1] for k in order], peak)
    scaled_out, peak = call(scale_kernel, "scale", [vmem] * 3, [flat, line])(response, peak, far)
    return (scaled_out, peak.reshape(span), gradients, filter_grad.reshape(channels, span))


def solution(mesh):
    return jax.shard_map(
        body,
        mesh=mesh,
        in_specs=(
            P(None, "ch", "ctx"),
            P(None, "ch", "ctx"),
            P("ch", None),
            P("ch"),
            P("ch"),
            P("ch", "ctx"),
        ),
        out_specs=(P("ch", "ctx"), P("ctx"), P(None, "ch", "ctx"), P("ch", "ctx")),
        check_vma=False,
    )
```
